32 devices in a mesh: row: 4 (over y, x), col: 2 (over core), scan: 4 (over z).
Axes of the slice: x: 2, y: 2, z: 4, core: 2. Of those that a mesh axis runs over, the one named last changes fastest.
Arguments:
- object_field: float32 [2, 2, 2048, 1024], P(None, None, 'row', 'col'), may hold values from -6 to 6
- probe_field: float32 [2, 256, 256], replicated, may hold values from -6 to 6
- prop_phase: float32 [256, 256], replicated, may hold values from -3.140625 to 3.140625
- measured: float32 [4, 2, 4, 3, 256, 256], P('row', 'col', 'scan'), may hold values from 0.3 to 3
- positions: int32 [4, 2, 4, 3, 2], P('row', 'col', 'scan'), may hold values from -64 to 320, as said below
- counts: int32 [4, 2, 4], P('row', 'col', 'scan'), may hold values from 1 to 3, as said below
Outputs:
- object_grad: float32 [2, 2, 2048, 1024], P(None, None, ('row', 'scan'), 'col')
The draws below stay inside these ranges and needn't reach their ends.
Inputs may be any that keep to these rules, and one draw needn't show every extreme that they name: `positions`: every patch lies inside the object; slots at and past the device's count are unused. `counts`: loads are uneven: some devices hold 3 patches while others of the same tile hold one.
All inputs are finite; a program needn't handle non-finite values.
Results may differ from the reference program's by a relative error of at most 0.018.
Values sent between devices are 32-bit elements; how exact they have to be, the bound alone decides.
No kernel may reach another device: no remote copies, remote signals or barrier semaphores. Data moves between devices by JAX's collectives and lax.ppermute only.
A program may use at most 64 MiB of HBM per device.

```python
import math
import jax
import jax.numpy as jnp
from jax import lax

PATCH = 256
TILE = 512
HALO = 64
PMAX = 3
ROWT = 4
COLT = 2
SHARDS = 4
NR = 2048
NC = 1024


def draw_positions(key, part):
    grid_shape = (ROWT, COLT, SHARDS, PMAX)
    first_key, second_key = jax.random.split(jax.random.fold_in(key, 17))
    upper_bound = TILE + HALO - PATCH
    tile_rows = jnp.arange(ROWT, dtype=jnp.int32)[:, None, None, None]
    tile_cols = jnp.arange(COLT, dtype=jnp.int32)[None, :, None, None]
    low_rows = jnp.broadcast_to(jnp.where(tile_rows == 0, 0, -HALO), grid_shape)
    high_rows = jnp.broadcast_to(jnp.where(tile_rows == ROWT - 1, TILE - PATCH, upper_bound), grid_shape)
    low_cols = jnp.broadcast_to(jnp.where(tile_cols == 0, 0, -HALO), grid_shape)
    high_cols = jnp.broadcast_to(jnp.where(tile_cols == COLT - 1, TILE - PATCH, upper_bound), grid_shape)
    row_offsets = jax.random.randint(first_key, grid_shape, low_rows, high_rows + 1, dtype=jnp.int32)
    col_offsets = jax.random.randint(second_key, grid_shape, low_cols, high_cols + 1, dtype=jnp.int32)
    row_offsets = row_offsets.at[0, 0, 0, 0].set(upper_bound).at[ROWT - 1, COLT - 1, 0, 0].set(-HALO)
    col_offsets = col_offsets.at[0, 0, 0, 0].set(upper_bound).at[ROWT - 1, COLT - 1, 0, 0].set(-HALO)
    return jnp.stack([row_offsets, col_offsets], -1)


def draw_counts(key, part):
    half_count = SHARDS // 2
    half_shape = (ROWT, COLT, half_count)
    heavy_key, side_key, middle_key = jax.random.split(jax.random.fold_in(key, 29), 3)
    heavy_pair = jax.random.randint(heavy_key, half_shape, 0, 2, dtype=jnp.int32)
    heavy_pair = heavy_pair.at[0, 0, 0].set(1)
    heavy_side = jax.random.randint(side_key, half_shape, 0, 2, dtype=jnp.int32)
    moderate = jax.random.randint(middle_key, (ROWT, COLT, SHARDS), 1, PMAX, dtype=jnp.int32)
    lower_heavy = jnp.where(heavy_side == 0, PMAX, 1)
    upper_heavy = jnp.where(heavy_side == 0, 1, PMAX)
    lower_half = jnp.where(heavy_pair == 1, lower_heavy, moderate[:, :, :half_count])
    upper_half = jnp.where(heavy_pair == 1, upper_heavy, moderate[:, :, half_count:])
    return jnp.concatenate([lower_half, upper_half], -1).astype(jnp.int32)


def shard_levels(stream_key, dims, cuts, smallest, top_value):
    factor_of = 1.0
    for dim, blocks in cuts:
        heights = jax.random.uniform(jax.random.fold_in(jax.random.fold_in(stream_key, 6), dim), (blocks,), jnp.float32, smallest / len(cuts), top_value / len(cuts))
        factor_of = factor_of * jnp.repeat(jnp.exp(heights), dims[dim] // blocks).reshape((-1,) + (1,) * (len(dims) - 1 - dim))
    return factor_of


def normal_values(key, shape, width, reach, cuts=(), held_as=jnp.bfloat16):
    result = jax.random.normal(key, shape, jnp.float32) * width
    if len(cuts) > 0:
        result = shard_levels(key, shape, cuts, -0.22, 0.18) * result
    return jnp.clip(result, min=-reach, max=reach).astype(held_as)


def setup_inputs(seed: int = 0) -> dict:
    arg_keys = jax.random.split(jax.random.key(seed), 7)
    object_field = normal_values(arg_keys[0], (2, 2, NR, NC), 0.7, 6.0, ((2, 4), (3, 2)), jnp.float32)
    probe_field = normal_values(arg_keys[1], (2, PATCH, PATCH), 0.7, 6.0, (), jnp.float32)
    prop_phase = jnp.clip(jax.random.uniform(arg_keys[2], (PATCH, PATCH), jnp.float32, -3.140625, 3.140625), -3.140625, 3.140625)
    measured = jnp.clip(jnp.exp(math.log(3.0) - 2.3025851 * jax.random.uniform(arg_keys[3], (ROWT, COLT, SHARDS, PMAX, PATCH, PATCH), jnp.float32) ** shard_levels(arg_keys[3], (ROWT, COLT, SHARDS, PMAX, PATCH, PATCH), ((0, 4), (1, 2), (2, 4)), -0.2, 0.2)), 0.3, 3.0)
    positions = draw_positions(jax.random.fold_in(arg_keys[6], 71), 0)
    counts = draw_counts(jax.random.fold_in(arg_keys[6], 71), 0)
    return {"object_field": object_field, "probe_field": probe_field, "prop_phase": prop_phase, "measured": measured, "positions": positions, "counts": counts}


def dft_tables(length):
    index_line = jnp.arange(length, dtype=jnp.int32)
    product = index_line[:, None] * index_line[None, :] % length
    angles = product.astype(jnp.float32) * (2.0 * math.pi / length)
    cosines = jnp.cos(angles) / math.sqrt(length)
    sines = jnp.sin(angles) / math.sqrt(length)
    left_fwd = jnp.stack([jnp.stack([cosines, sines], 1), jnp.stack([-sines, cosines], 1)], 0)
    right_fwd = jnp.stack([jnp.stack([cosines, -sines], 1), jnp.stack([sines, cosines], 1)], 0)
    left_inv = jnp.stack([jnp.stack([cosines, -sines], 1), jnp.stack([sines, cosines], 1)], 0)
    right_inv = jnp.stack([jnp.stack([cosines, sines], 1), jnp.stack([-sines, cosines], 1)], 0)
    return (left_fwd.astype(jnp.bfloat16), right_fwd.astype(jnp.bfloat16), left_inv.astype(jnp.bfloat16), right_inv.astype(jnp.bfloat16))

def transform(values, left_table, right_table):
    middle = jnp.einsum('qapb,pbc->qac', left_table.astype(jnp.float32), values.astype(jnp.float32), precision=lax.Precision.HIGHEST)
    middle = middle.astype(jnp.bfloat16)
    return jnp.einsum('pab,pbqc->qac', middle.astype(jnp.float32), right_table.astype(jnp.float32), precision=lax.Precision.HIGHEST)

def complex_mul(first, second):
    return jnp.stack([first[0] * second[0] - first[1] * second[1], first[0] * second[1] + first[1] * second[0]])

def conj_mul(first, second):
    return jnp.stack([first[0] * second[0] + first[1] * second[1], first[0] * second[1] - first[1] * second[0]])

def patch_grads(first_slice, second_slice, probe_field, propagator, intensity, tables):
    left_fwd, right_fwd, left_inv, right_inv = tables
    entrance = complex_mul(probe_field, first_slice).astype(jnp.bfloat16)
    spectrum = complex_mul(propagator, transform(entrance, left_fwd, right_fwd)).astype(jnp.bfloat16)
    arrived = transform(spectrum, left_inv, right_inv)
    leaving = complex_mul(second_slice, arrived).astype(jnp.bfloat16)
    far_field = transform(leaving, left_fwd, right_fwd)
    power = far_field[0] * far_field[0] + far_field[1] * far_field[1]
    residual = ((power - intensity)[None] * far_field).astype(jnp.bfloat16)
    back_second = transform(residual, left_inv, right_inv)
    grad_second = conj_mul(arrived, back_second)
    through = conj_mul(second_slice, back_second).astype(jnp.bfloat16)
    back_spectrum = conj_mul(propagator, transform(through, left_fwd, right_fwd)).astype(jnp.bfloat16)
    back_first = transform(back_spectrum, left_inv, right_inv)
    grad_first = conj_mul(probe_field, back_first)
    return jnp.stack([grad_first, grad_second])

def reference(object_field, probe_field, prop_phase, measured, positions, counts):
    tables = dft_tables(PATCH)
    propagator = jnp.stack([jnp.cos(prop_phase), jnp.sin(prop_phase)])
    padded = jnp.pad(object_field, ((0, 0), (0, 0), (HALO, HALO), (HALO, HALO)))
    gradient = jnp.zeros(padded.shape, jnp.float32)
    tile_rows, tile_cols, shard_count = counts.shape
    grid_shape = (tile_rows, tile_cols, shard_count, PMAX)
    row_index = jnp.broadcast_to(jnp.arange(tile_rows, dtype=jnp.int32)[:, None, None, None], grid_shape).reshape(-1)
    col_index = jnp.broadcast_to(jnp.arange(tile_cols, dtype=jnp.int32)[None, :, None, None], grid_shape).reshape(-1)
    slot_index = jnp.broadcast_to(jnp.arange(PMAX, dtype=jnp.int32)[None, None, None, :], grid_shape)
    live_slot = (slot_index < counts[..., None]).reshape(-1)
    corners = positions.reshape(-1, 2).astype(jnp.int32)
    intensities = measured.reshape(-1, PATCH, PATCH)
    zero_index = jnp.zeros((), jnp.int32)

    def scan_step(carry, item):
        tile_row, tile_col, corner, on_flag, intensity = item
        row_start = (tile_row * TILE + corner[0] + HALO).astype(jnp.int32)
        col_start = (tile_col * TILE + corner[1] + HALO).astype(jnp.int32)
        starts = (zero_index, zero_index, row_start, col_start)

        def one_patch(current):
            window = lax.dynamic_slice(padded, starts, (2, 2, PATCH, PATCH))
            update = patch_grads(window[0], window[1], probe_field, propagator, intensity, tables)
            present = lax.dynamic_slice(current, starts, (2, 2, PATCH, PATCH))
            return lax.dynamic_update_slice(current, present + update, starts)

        def unchanged(current):
            return current
        return (lax.cond(on_flag, one_patch, unchanged, carry), None)
    gradient, _ = lax.scan(scan_step, gradient, (row_index, col_index, corners, live_slot, intensities))
    return gradient[:, :, HALO:-HALO, HALO:-HALO]
```

```python
import functools
import math

import jax
import jax.numpy as jnp
import numpy as np
from jax import lax
from jax.experimental import pallas as pl
from jax.experimental.pallas import tpu as pltpu
from jax.sharding import PartitionSpec as P

PATCH = 256
HALO = 64
PMAX = 3
LANE = 128
VMEM_LIMIT = 32 * 1024 * 1024
VMEM_LITTLE = 8 * 1024 * 1024
NOTE_ROWS = 8


def block_tables():
    line = np.arange(PATCH)
    angles = (line[:, None] * line[None, :] % PATCH) * (2.0 * math.pi / PATCH)
    cosines = np.cos(angles) / math.sqrt(PATCH)
    sines = np.sin(angles) / math.sqrt(PATCH)
    turn = np.block([[cosines, sines], [-sines, cosines]])
    back = np.block([[cosines, -sines], [sines, cosines]])
    return (jnp.asarray(turn.astype(np.float32)).astype(jnp.bfloat16), jnp.asarray(back.astype(np.float32)).astype(jnp.bfloat16))


def pair_of(index, phase):
    return index + 1 if index % 2 == phase else index - 1


def pairings(size):
    return range(1 if size <= 2 else 2)


def joint_permute(value, names, targets):
    sizes = [lax.axis_size(name) for name in names]
    route = []
    for flat in range(math.prod(sizes)):
        place = np.unravel_index(flat, sizes)
        goal = targets(*[int(i) for i in place])
        if goal is None or any(not 0 <= g < s for g, s in zip(goal, sizes)):
            continue
        route.append((flat, int(np.ravel_multi_index(goal, sizes))))
    return lax.ppermute(value, tuple(names) if len(names) > 1 else names[0], route)


OUTER = -1


def transform(pairs, left, right):
    stacked = jnp.concatenate(
        [jnp.concatenate([pair[part] for pair in pairs], axis=1) for part in range(2)], axis=0
    )
    middle = jnp.dot(left[...], stacked, preferred_element_type=jnp.float32).astype(jnp.bfloat16)
    size = PATCH
    middle = jnp.concatenate(
        [
            jnp.concatenate(
                [middle[p * size : (p + 1) * size, i * size : (i + 1) * size] for p in range(2)],
                axis=1,
            )
            for i in range(len(pairs))
        ],
        axis=0,
    )
    result = jnp.dot(middle, right[...], preferred_element_type=jnp.float32)
    return [
        (
            result[i * size : (i + 1) * size, :size],
            result[i * size : (i + 1) * size, size:],
        )
        for i in range(len(pairs))
    ]


def rounded(pair):
    return pair[0].astype(jnp.bfloat16), pair[1].astype(jnp.bfloat16)


def product(a, b):
    return a[0] * b[0] - a[1] * b[1], a[0] * b[1] + a[1] * b[0]


def conj_product(a, b):
    return a[0] * b[0] + a[1] * b[1], a[0] * b[1] - a[1] * b[0]


def lanes():
    return lax.broadcasted_iota(jnp.int32, (PATCH, LANE), 1)


def corner_of(row, col):
    return row + HALO, (col + LANE) // LANE, lax.rem(col + LANE, LANE)


def window(ext, slice_at, row, col):
    top, tile, shift = corner_of(row, col)
    turn = lax.rem(LANE - shift, LANE)
    inside = lanes() < LANE - shift

    def plane(index):
        moved = [
            pltpu.roll(ext[index, tile + j, pl.ds(top, PATCH), :], turn, 1) for j in range(3)
        ]
        return jnp.concatenate([jnp.where(inside, moved[j], moved[j + 1]) for j in range(2)], axis=1)

    return plane(2 * slice_at), plane(2 * slice_at + 1)


def deposit(acc, slice_at, row, col, pair):
    top, tile, shift = corner_of(row, col)
    inside = lanes() >= shift
    blank = jnp.zeros((PATCH, LANE), jnp.float32)
    for part in range(2):
        moved = [
            pltpu.roll(pair[part][:, j * LANE : (j + 1) * LANE], shift, 1) for j in range(2)
        ]
        moved = [blank, *moved, blank]
        for j in range(3):
            acc[2 * slice_at + part, tile + j, pl.ds(top, PATCH), :] += jnp.where(
                inside, moved[j + 1], moved[j]
            )


def forward(ext, corners, probe, wave, turn, back):
    lamp = (probe[0], probe[1])
    prop = (wave[0][...], wave[1][...])
    entrance = [rounded(product(lamp, window(ext, 0, *corner))) for corner in corners]
    spectra = transform(entrance, turn, back)
    arrived = transform([rounded(product(prop, x)) for x in spectra], back, turn)
    seconds = [window(ext, 1, *corner) for corner in corners]
    far = transform([rounded(product(o, w)) for o, w in zip(seconds, arrived)], turn, back)
    return far, arrived, seconds


def backward(far, arrived, seconds, intensities, probe, wave, turn, back, put):
    lamp = (probe[0], probe[1])
    prop = (wave[0][...], wave[1][...])
    residuals = []
    for psi, intensity in zip(far, intensities):
        misfit = psi[0] * psi[0] + psi[1] * psi[1] - intensity
        residuals.append(rounded((misfit * psi[0], misfit * psi[1])))
    back_seconds = transform(residuals, back, turn)
    for i, (w, g) in enumerate(zip(arrived, back_seconds)):
        put(i, 1, conj_product(w, g))
    through = [rounded(conj_product(o, g)) for o, g in zip(seconds, back_seconds)]
    spectra = transform(through, turn, back)
    back_firsts = transform([rounded(conj_product(prop, x)) for x in spectra], back, turn)
    for i, g in enumerate(back_firsts):
        put(i, 0, conj_product(lamp, g))


def place_of(height):
    shard_count = lax.axis_size("scan")
    scan_at = lax.axis_index("scan")
    band = height // shard_count
    upper = scan_at < shard_count // 2
    even = scan_at % 2 == 0
    open_at = jnp.where(upper, HALO, 0)
    shut_at = jnp.where(upper, 0, band - HALO)
    other_at = jnp.where(even, band, 0)
    return [
        jnp.where(upper, 0, height // 2),
        jnp.where(upper, height, -HALO),
        lax.axis_index("row") % 2,
        lax.axis_index("col") % 2,
        jnp.where(even, 0, band),
        other_at + open_at,
        other_at + shut_at,
        ((scan_at == 0) | (scan_at == shard_count - 1)).astype(jnp.int32),
        shut_at,
        open_at,
    ]


def wanted(place, row, half_rows):
    inner = (row < place[0] + half_rows) & (row + PATCH > place[0])
    outer = (row < place[1] + HALO) & (row + PATCH > place[1])
    return inner | outer


def far_tile(place, phase, tiles):
    return jnp.where(place[3] == phase, tiles - 1, 0)


class Copies:
    def __init__(self, sems):
        self.sems, self.all = sems, []

    def start(self, source, target):
        copy = pltpu.make_async_copy(source, target, self.sems.at[len(self.all)])
        copy.start()
        self.all.append(copy)
        return copy

    def wait(self):
        for copy in self.all:
            copy.wait()


def staging_kernel(sides, core, *refs):
    col_refs, refs = refs[:sides], refs[sides:]
    near, (ext, *near_to), sems = refs[:4], refs[4:-1], refs[-1]
    height, width = core.shape[1], core.shape[2]
    tiles = ext.shape[1]
    place = place_of(height)
    copies = Copies(sems)
    for t in range(width // LANE):
        part = core.at[:, :, pl.ds(t * LANE, LANE)]
        copies.start(part, ext.at[:, t + 1, pl.ds(HALO, height), :])
    for j, ref in enumerate(col_refs):
        copies.start(ref, ext.at[:, far_tile(place, j, tiles), pl.ds(HALO, height), :])
    for source, target in zip(near, near_to):
        copies.start(source, target)
    copies.wait()


def patches_kernel(sides, cuts, peer, *refs):
    row_refs, refs = refs[: sides[0]], refs[sides[0] :]
    corner_refs, refs = refs[: sides[0] * sides[1]], refs[sides[0] * sides[1] :]
    own_corners, own_count, ext, own, probe, cosine, sine, turn, back = refs[:9]
    outs, (acc, note, queue, sems) = refs[10:-4], refs[-4:]
    wave = (cosine, sine)
    tiles, height = ext.shape[1], ext.shape[2] - 2 * HALO
    half_rows = height // 2
    place = place_of(height)
    copies = Copies(sems)

    def far_row(phase):
        return pl.multiple_of(jnp.where(place[2] == phase, height + HALO, 0), 8)

    for i, ref in enumerate(row_refs):
        for t in range(tiles - 2):
            part = ref.at[:, :, pl.ds(t * LANE, LANE)]
            copies.start(part, ext.at[:, t + 1, pl.ds(far_row(i), HALO), :])
    for k, ref in enumerate(corner_refs):
        i, j = divmod(k, sides[1])
        copies.start(ref, ext.at[:, far_tile(place, j, tiles), pl.ds(far_row(i), HALO), :])
    note_at = pl.ds(PMAX * PATCH, NOTE_ROWS)
    copies.start(peer.at[note_at, pl.ds(0, LANE)], note)
    first = pl.multiple_of(place[0] + HALO, 8)
    outer = pl.multiple_of(place[1] + HALO, 8)
    acc[:, :, pl.ds(first, half_rows), :] = jnp.zeros((4, tiles, half_rows, LANE), jnp.float32)
    acc[:, :, pl.ds(outer, HALO), :] = jnp.zeros((4, tiles, HALO, LANE), jnp.float32)

    def intensity(index):
        mine = own[jnp.minimum(index, PMAX - 1)]
        start = pl.multiple_of(jnp.maximum(index - PMAX, 0) * PATCH, PATCH)
        return jnp.where(index < PMAX, mine, peer[pl.ds(start, PATCH), :])

    copies.wait()
    length = jnp.int32(0)
    for index in range(2 * PMAX):
        slot = index % PMAX
        if index < PMAX:
            row, col, count = own_corners[slot, 0], own_corners[slot, 1], own_count[0]
        else:
            row, col, count = [
                note[0, at].astype(jnp.int32) for at in (2 * slot, 2 * slot + 1, 2 * PMAX)
            ]
        queue[3 * length] = index
        queue[3 * length + 1] = row
        queue[3 * length + 2] = col
        length = length + ((slot < count) & wanted(place, row, half_rows)).astype(jnp.int32)

    def step(turn_at, carry):
        items = [2 * turn_at, jnp.minimum(2 * turn_at + 1, length - 1)]
        whole = 2 * turn_at + 1 < length
        corners = [(queue[3 * i + 1], queue[3 * i + 2]) for i in items]
        far, arrived, seconds = forward(ext, corners, probe, wave, turn, back)

        def put(i, slice_at, pair):
            if i == 0:
                deposit(acc, slice_at, *corners[i], pair)
            else:
                pl.when(whole)(lambda: deposit(acc, slice_at, *corners[i], pair))

        intensities = [intensity(queue[3 * i]) for i in items]
        backward(far, arrived, seconds, intensities, probe, wave, turn, back, put)
        return carry

    lax.fori_loop(0, (length + 1) // 2, step, 0)
    gifts = Copies(sems)
    for target, parts in zip(outs, cuts):
        row_to = 0
        for tile, at, count in parts:
            tile = far_tile(place, tile[0], tiles) if isinstance(tile, tuple) else tile
            row = outer if at == OUTER else first
            row = row if at in (OUTER, None) else pl.multiple_of(first + place[at], 8)
            gifts.start(
                acc.at[:, pl.ds(tile, target.shape[1]), pl.ds(row, count), :],
                target.at[:, :, pl.ds(row_to, count), :],
            )
            row_to += count
    gifts.wait()


def near_tile(place, phase, tiles):
    return jnp.where(place[3] == phase, tiles - 1, 0)


def add_rims(place, out, rims, rim_row):
    _, tiles, rows, _ = out.shape
    for j, rim in enumerate(rims):
        at = near_tile(place, j, tiles)
        out[:, at, :, :] += rim[:, 0, pl.ds(rim_row, rows), :]


def edge_kernel(height, sides, open_left, open_right, outer_left, outer_right, *refs):
    place = place_of(height)
    rims, (open_out, outer_out) = refs[:sides], refs[-2:]
    open_out[:, 0:1] = open_left[...]
    open_out[:, 1:2] = open_right[...]
    add_rims(place, open_out, rims, pl.multiple_of(place[5], 8))
    outer_out[:, 0:1] = outer_left[...]
    outer_out[:, 1:2] = outer_right[...]
    add_rims(place, outer_out, rims, height // 2)


def shut_inner_kernel(height, part, strip, out):
    place = place_of(height)
    out[...] = part[...]

    @pl.when(place[7] == 0)
    def _():
        out[...] += strip[...]


def shut_edge_kernel(height, sides, left, right, strip, *refs):
    place = place_of(height)
    rims, out = refs[:sides], refs[sides]
    out[:, 0:1] = left[...]
    out[:, 1:2] = right[...]
    add_rims(place, out, rims, pl.multiple_of(place[6], 8))

    @pl.when(place[7] == 0)
    def _():
        out[...] += strip[...]


def final_kernel(height, sides, part, *refs):
    place = place_of(height)
    open_got, shut_got, strip, rims = refs[:2], refs[2:4], refs[4:6], refs[6 : 6 + sides]
    out, work = refs[6 + sides :]
    work[...] = part[...]
    tiles = work.shape[1]
    add_rims(place, work, rims, pl.multiple_of(place[4], 8))

    def add(at, inner, edge):
        rows = pl.ds(pl.multiple_of(at, 8), inner.shape[2])
        work[:, 1 : tiles - 1, rows, :] += inner[...]
        work[:, 0:1, rows, :] += edge[:, 0:1]
        work[:, tiles - 1 : tiles, rows, :] += edge[:, 1:2]

    add(place[9], *open_got)
    add(place[8], *shut_got)

    @pl.when(place[7] == 1)
    def _():
        add(place[8], *strip)

    for t in range(tiles):
        out[:, :, t * LANE : (t + 1) * LANE] = work[:, t]


def half_kernel(height, sides, part, inner, edge, *refs):
    place = place_of(height)
    rims, out = refs[:sides], refs[sides]
    out[...] = part[...]
    add_rims(place, out, rims, 0)
    tiles = out.shape[1]
    rows = pl.ds(pl.multiple_of(jnp.where(place[0] == 0, 0, out.shape[2] - HALO), 8), HALO)
    out[:, 1 : tiles - 1, rows, :] += inner[...]
    out[:, 0:1, rows, :] += edge[:, 0:1]
    out[:, tiles - 1 : tiles, rows, :] += edge[:, 1:2]


def near_rows(place, phase, height):
    return pl.ds(pl.multiple_of(jnp.where(place[2] == phase, height - HALO, 0), HALO), HALO)


def near_cols(place, phase, width):
    return pl.ds(pl.multiple_of(jnp.where(place[3] == phase, width - LANE, 0), LANE), LANE)


def note_kernel(corners, count, own, out, sems):
    copies = Copies(sems)
    for slot in range(PMAX):
        copies.start(own.at[slot], out.at[pl.ds(slot * PATCH, PATCH), :])
    lane = lax.broadcasted_iota(jnp.int32, (NOTE_ROWS, PATCH), 1)
    values = jnp.where(lane == 2 * PMAX, count[0], 0)
    for index in range(2 * PMAX):
        values = jnp.where(lane == index, corners[index // 2, index % 2], values)
    out[PMAX * PATCH :, :] = values.astype(jnp.float32)
    copies.wait()


def columns_kernel(core, *refs):
    outs, copies = refs[:-1], Copies(refs[-1])
    place = place_of(core.shape[1])
    for j, out in enumerate(outs):
        copies.start(core.at[:, :, near_cols(place, j, core.shape[2])], out)
    copies.wait()


def rows_kernel(sides, core, *refs):
    outs, copies = refs[:-1], Copies(refs[-1])
    height, width = core.shape[1:]
    place = place_of(height)
    for i in range(sides[0]):
        rows = near_rows(place, i, height)
        copies.start(core.at[:, rows, :], outs[i])
        for j in range(sides[1]):
            target = outs[sides[0] + i * sides[1] + j]
            copies.start(core.at[:, rows, near_cols(place, j, width)], target)
    copies.wait()


ANY = pl.BlockSpec(memory_space=pl.ANY)
VMEM = pl.BlockSpec(memory_space=pltpu.VMEM)
SMEM = pl.BlockSpec(memory_space=pltpu.SMEM)


def block(*shape):
    return jax.ShapeDtypeStruct(shape, jnp.float32)


def call(kernel, out_shapes, in_specs, out_specs, scratch, *operands, limit=VMEM_LIMIT, aliases=None):
    return pl.pallas_call(
        kernel,
        out_shape=out_shapes,
        in_specs=in_specs,
        out_specs=out_specs,
        scratch_shapes=scratch,
        input_output_aliases=aliases or {},
        compiler_params=pltpu.CompilerParams(vmem_limit_bytes=limit),
        cost_estimate=pl.CostEstimate(flops=0, bytes_accessed=0, transcendentals=0),
    )(*operands)


def shards(object_field, probe_field, prop_phase, measured, positions, counts):
    height, width = object_field.shape[2:]
    shard_count = lax.axis_size("scan")
    half_rows = height // 2
    band = height // shard_count
    rest = band - HALO
    tiles = width // LANE
    row_sides = pairings(lax.axis_size("row"))
    col_sides = pairings(lax.axis_size("col"))
    sides = len(col_sides)
    both = (len(row_sides), sides)
    stride = shard_count // 2
    scan_at = lax.axis_index("scan")
    planes = object_field.reshape(4, height, width)
    own = measured.reshape(PMAX, PATCH, PATCH)
    own_corners, own_count = positions.reshape(PMAX, 2), counts.reshape(1)

    def across(value):
        return lax.ppermute(value, "scan", [(i, i ^ stride) for i in range(shard_count)])

    def to_cols(value, j):
        return joint_permute(value, ("col",), lambda c: (pair_of(c, j),))

    def to_rows(value, i):
        return joint_permute(value, ("row",), lambda r: (pair_of(r, i),))

    def to_corner(value, i, j):
        return joint_permute(value, ("row", "col"), lambda r, c: (pair_of(r, i), pair_of(c, j)))

    def cut_edges(kernel, shapes):
        return call(
            kernel,
            shapes,
            [ANY],
            [VMEM] * len(shapes),
            [pltpu.SemaphoreType.DMA((len(shapes),))],
            planes,
            limit=VMEM_LITTLE,
        )

    noted = call(
        note_kernel,
        block(PMAX * PATCH + NOTE_ROWS, PATCH),
        [SMEM, SMEM, ANY],
        VMEM,
        [pltpu.SemaphoreType.DMA((PMAX,))],
        own_corners,
        own_count,
        own,
        limit=VMEM_LITTLE,
    )
    peer = across(noted)
    row_edges = cut_edges(
        functools.partial(rows_kernel, both),
        [block(4, HALO, width)] * both[0] + [block(4, HALO, LANE)] * (both[0] * sides),
    )
    row_halos = [to_rows(row_edges[i], i) for i in row_sides]
    col_edges = cut_edges(columns_kernel, [block(4, height, LANE)] * sides)
    col_halos = [to_cols(edge, j) for j, edge in zip(col_sides, col_edges)]
    corner_halos = [
        to_corner(row_edges[both[0] + i * sides + j], i, j) for i in row_sides for j in col_sides
    ]
    cosine, sine = jnp.cos(prop_phase), jnp.sin(prop_phase)
    turn, back = block_tables()

    two_bands = shard_count == 4 and rest > 0
    inner = tiles - 2
    cuts = [(inner, [(2, OUTER, HALO)]), (1, [(1, OUTER, HALO)]), (1, [(tiles, OUTER, HALO)])]
    cuts += [(1, [((j,), None, half_rows), ((j,), OUTER, HALO)]) for j in col_sides]
    if two_bands:
        for at, rows in ((5, rest), (6, HALO)):
            cuts += [(inner, [(2, at, rows)]), (1, [(1, at, rows)]), (1, [(tiles, at, rows)])]
        cuts += [(tiles, [(1, 4, band)])]
    else:
        cuts += [(tiles, [(1, None, half_rows)]), (1, [(1, None, HALO)]), (1, [(1, None, HALO)])]
    full = (4, tiles + 2, height + 2 * HALO, LANE)
    table = jax.ShapeDtypeStruct(turn.shape, turn.dtype)
    staged = call(
        functools.partial(staging_kernel, sides),
        [block(*full), block(*own.shape), block(*probe_field.shape), table, table],
        [ANY] * (sides + 5),
        [VMEM] * 5,
        [pltpu.SemaphoreType.DMA((tiles + sides + 4,))],
        planes,
        *col_halos,
        own,
        probe_field,
        turn,
        back,
        limit=VMEM_LITTLE,
    )
    ext, own, lamp, turn, back = staged
    arrivals = [peer, *row_halos, *corner_halos]
    copy_count = max(
        (tiles + sides) * both[0] + 1, sum(len(parts) for _, parts in cuts)
    )
    outs = call(
        functools.partial(patches_kernel, both, [parts for _, parts in cuts]),
        [block(*full)] + [block(4, wide, sum(part[2] for part in parts), LANE) for wide, parts in cuts],
        [VMEM] + [ANY] * (len(arrivals) - 1) + [SMEM, SMEM] + [VMEM] * 7,
        [VMEM] + [ANY] * len(cuts),
        [
            pltpu.VMEM(full, jnp.float32),
            pltpu.SMEM((NOTE_ROWS, LANE), jnp.float32),
            pltpu.SMEM((3 * (2 * PMAX + 1),), jnp.int32),
            pltpu.SemaphoreType.DMA((copy_count,)),
        ],
        *arrivals,
        own_corners,
        own_count,
        ext,
        own,
        lamp,
        cosine,
        sine,
        turn,
        back,
        aliases={len(arrivals) + 2: 0},
    )[1:]
    outer_inner, outer_left, outer_right = outs[:3]
    rims, pieces = outs[3 : 3 + sides], outs[3 + sides :]

    def to_next(value):
        return joint_permute(
            value, ("row", "scan"), lambda r, s: (r + 1 if s < stride else r - 1, s)
        )

    def beside(value, mask=1):
        return lax.ppermute(value, "scan", [(i, i ^ mask) for i in range(shard_count)])

    def fold(kernel, out_shapes, *operands, scratch=()):
        many = isinstance(out_shapes, tuple)
        return call(
            functools.partial(kernel, height),
            out_shapes,
            [VMEM] * len(operands),
            (VMEM,) * len(out_shapes) if many else VMEM,
            list(scratch),
            *operands,
            limit=VMEM_LITTLE,
        )

    got_rims = [to_cols(rim, j) for j, rim in zip(col_sides, rims)]
    got_inner = to_next(outer_inner)
    open_edge, outer_edge = fold(
        lambda *refs: edge_kernel(refs[0], sides, *refs[1:]),
        (block(4, 2, pieces[1].shape[2], LANE), block(4, 2, HALO, LANE)),
        pieces[1],
        pieces[2],
        outer_left,
        outer_right,
        *got_rims,
    )
    got_edge = to_next(outer_edge)
    if not two_bands:
        half = fold(
            lambda *refs: half_kernel(refs[0], sides, *refs[1:]),
            block(4, tiles, half_rows, LANE),
            pieces[0],
            got_inner,
            got_edge,
            *got_rims,
        )
        mask = stride // 2
        while mask > 0:
            size = half.shape[2] // 2
            low = (scan_at & mask) == 0
            keep = lax.dynamic_slice_in_dim(half, jnp.where(low, 0, size), size, axis=2)
            send = lax.dynamic_slice_in_dim(half, jnp.where(low, size, 0), size, axis=2)
            half = keep + beside(send, mask)
            mask //= 2
        return half.transpose(0, 2, 1, 3).reshape(2, 2, band, width)
    got_open = [beside(pieces[0]), beside(open_edge)]
    got_inner, *got_open = lax.optimization_barrier((got_inner, *got_open))
    shut_inner = fold(shut_inner_kernel, block(4, inner, HALO, LANE), pieces[3], got_inner)
    got_shut = [beside(shut_inner)]
    shut_edge = fold(
        lambda *refs: shut_edge_kernel(refs[0], sides, *refs[1:]),
        block(4, 2, HALO, LANE),
        pieces[4],
        pieces[5],
        got_edge,
        *got_rims,
    )
    got_shut.append(beside(shut_edge))
    total = fold(
        lambda *refs: final_kernel(refs[0], sides, *refs[1:]),
        block(4, band, width),
        pieces[6],
        *got_open,
        *got_shut,
        got_inner,
        got_edge,
        *got_rims,
        scratch=[pltpu.VMEM((4, tiles, band, LANE), jnp.float32)],
    )
    return total.reshape(2, 2, band, width)


def solution(mesh):
    placed = (
        P(None, None, "row", "col"),
        P(),
        P(),
        P("row", "col", "scan", None, None, None),
        P("row", "col", "scan", None, None),
        P("row", "col", "scan"),
    )
    return jax.shard_map(
        shards,
        mesh=mesh,
        in_specs=placed,
        out_specs=P(None, None, ("row", "scan"), "col"),
        check_vma=False,
    )
```

```python
import functools
import math

import jax
import jax.numpy as jnp
import numpy as np
from jax import lax
from jax.experimental import pallas as pl
from jax.experimental.pallas import tpu as pltpu
from jax.sharding import PartitionSpec as P

PATCH = 256
HALO = 64
PMAX = 3
LANE = 128
HALF = PATCH // 2
VMEM_LIMIT = 32 * 1024 * 1024
VMEM_LITTLE = 8 * 1024 * 1024
GROUP = 4


def block_tables():
    index = np.arange(HALF)
    tables = []
    for odd in range(2):
        angles = ((2 * index[:, None] + odd) * index[None, :] % PATCH) * (2.0 * math.pi / PATCH)
        cosines = np.cos(angles) / math.sqrt(PATCH)
        sines = np.sin(angles) / math.sqrt(PATCH)
        tables.append(np.block([[cosines, sines], [-sines, cosines]]))
    tables += [table.T for table in tables]
    return jnp.asarray(np.stack(tables).astype(np.float32)).astype(jnp.bfloat16)


def sorted_columns():
    index = np.arange(PATCH)
    matrix = np.zeros((PATCH, PATCH), np.float32)
    matrix[index, index % 2 * HALF + index // 2] = 1.0
    return jnp.asarray(np.stack([matrix, matrix.T])).astype(jnp.bfloat16)


def pair_of(index, phase):
    return index + 1 if index % 2 == phase else index - 1


def pairings(size):
    return range(1 if size <= 2 else 2)


def joint_permute(value, names, targets):
    sizes = [lax.axis_size(name) for name in names]
    route = []
    for flat in range(math.prod(sizes)):
        place = np.unravel_index(flat, sizes)
        goal = targets(*[int(i) for i in place])
        if goal is None or any(not 0 <= g < s for g, s in zip(goal, sizes)):
            continue
        route.append((flat, int(np.ravel_multi_index(goal, sizes))))
    return lax.ppermute(value, tuple(names) if len(names) > 1 else names[0], route)


OUTER = -1


def times(a, b):
    return jnp.dot(
        a.astype(jnp.bfloat16), b.astype(jnp.bfloat16), preferred_element_type=jnp.float32
    )


def side(parts, axis):
    return jnp.concatenate(parts, axis=axis)


def to_frequencies(pairs, tables):
    tall = []
    for odd in range(2):
        halves = [
            [x[:HALF] - x[HALF:] if odd else x[:HALF] + x[HALF:] for x in pair] for pair in pairs
        ]
        tall.append(times(tables[odd], side([side(half, 0) for half in halves], 1)))
    wide = []
    for odd in range(2):
        rows = []
        for i in range(len(pairs)):
            first, second = 2 * i * HALF, (2 * i + 1) * HALF
            for y in tall:
                parts = []
                for part in range(2):
                    x = y[part * HALF : (part + 1) * HALF]
                    low, high = x[:, first:second], x[:, second : second + HALF]
                    parts.append(low - high if odd else low + high)
                rows.append(side(parts, 1))
        wide.append(times(side(rows, 0), tables[2 + odd]))
    return [
        [(z[i * PATCH : (i + 1) * PATCH, :HALF], z[i * PATCH : (i + 1) * PATCH, HALF:]) for z in wide]
        for i in range(len(pairs))
    ]


def from_frequencies(spectra, tables):
    parts = []
    for odd in range(2):
        rows = slice(odd * HALF, (odd + 1) * HALF)
        columns = [side([x[rows] for x in pair], 0) for spectrum in spectra for pair in spectrum]
        parts.append(times(tables[2 + odd], side(columns, 1)))
    halves = [parts[0] + parts[1], parts[0] - parts[1]]
    sums = []
    for odd in range(2):
        rows = []
        for i in range(len(spectra)):
            at = (2 * i + odd) * HALF
            for half in halves:
                rows.append(side([half[:HALF, at : at + HALF], half[HALF:, at : at + HALF]], 1))
        sums.append(times(side(rows, 0), tables[odd]))
    low, high = sums[0] + sums[1], sums[0] - sums[1]
    results = []
    for i in range(len(spectra)):
        rows = slice(i * PATCH, (i + 1) * PATCH)
        results.append(
            tuple(side([x[rows, p * HALF : (p + 1) * HALF] for x in (low, high)], 1) for p in range(2))
        )
    return results


def product(a, b):
    return a[0] * b[0] - a[1] * b[1], a[0] * b[1] + a[1] * b[0]


def conj_product(a, b):
    return a[0] * b[0] + a[1] * b[1], a[0] * b[1] - a[1] * b[0]


def lanes():
    return lax.broadcasted_iota(jnp.int32, (PATCH, LANE), 1)


def corner_of(row, col):
    return row + HALO, (col + LANE) // LANE, lax.rem(col + LANE, LANE)


def window(ext, slice_at, row, col):
    top, tile, shift = corner_of(row, col)
    turn = lax.rem(LANE - shift, LANE)
    inside = lanes() < LANE - shift

    def plane(index):
        moved = [
            pltpu.roll(ext[index, tile + j, pl.ds(top, PATCH), :], turn, 1) for j in range(3)
        ]
        return jnp.concatenate([jnp.where(inside, moved[j], moved[j + 1]) for j in range(2)], axis=1)

    return plane(2 * slice_at), plane(2 * slice_at + 1)


def deposit(acc, slice_at, row, col, pair):
    top, tile, shift = corner_of(row, col)
    inside = lanes() >= shift
    blank = jnp.zeros((PATCH, LANE), jnp.float32)
    for part in range(2):
        moved = [
            pltpu.roll(pair[part][:, j * LANE : (j + 1) * LANE], shift, 1) for j in range(2)
        ]
        moved = [blank, *moved, blank]
        for j in range(3):
            acc[2 * slice_at + part, tile + j, pl.ds(top, PATCH), :] += jnp.where(
                inside, moved[j + 1], moved[j]
            )


def patch_gradients(ext, corners, intensities, probe, waves, tables, put):
    lamp = (probe[0], probe[1])
    prop = [(waves[0, odd], waves[1, odd]) for odd in range(2)]

    def through_prop(multiply, spectra):
        return [[multiply(h, z) for h, z in zip(prop, spectrum)] for spectrum in spectra]

    entrance = [product(lamp, window(ext, 0, *corner)) for corner in corners]
    arrived = from_frequencies(through_prop(product, to_frequencies(entrance, tables)), tables)
    seconds = [window(ext, 1, *corner) for corner in corners]
    far = to_frequencies([product(o, w) for o, w in zip(seconds, arrived)], tables)
    residuals = []
    for spectrum, intensity in zip(far, intensities):
        misfits = [z[0] * z[0] + z[1] * z[1] - i for z, i in zip(spectrum, intensity)]
        residuals.append([(m * z[0], m * z[1]) for m, z in zip(misfits, spectrum)])
    back_seconds = from_frequencies(residuals, tables)
    for i, (w, g) in enumerate(zip(arrived, back_seconds)):
        put(i, 1, conj_product(w, g))
    through = [conj_product(o, g) for o, g in zip(seconds, back_seconds)]
    back_spectra = through_prop(conj_product, to_frequencies(through, tables))
    for i, g in enumerate(from_frequencies(back_spectra, tables)):
        put(i, 0, conj_product(lamp, g))


def place_of(height):
    shard_count = lax.axis_size("scan")
    scan_at = lax.axis_index("scan")
    band = height // shard_count
    upper = scan_at < shard_count // 2
    even = scan_at % 2 == 0
    open_at = jnp.where(upper, HALO, 0)
    shut_at = jnp.where(upper, 0, band - HALO)
    other_at = jnp.where(even, band, 0)
    return [
        jnp.where(upper, 0, height // 2),
        jnp.where(upper, height, -HALO),
        lax.axis_index("row") % 2,
        lax.axis_index("col") % 2,
        jnp.where(even, 0, band),
        other_at + open_at,
        other_at + shut_at,
        ((scan_at == 0) | (scan_at == shard_count - 1)).astype(jnp.int32),
        shut_at,
        open_at,
    ]


def wanted(place, row, half_rows):
    inner = (row < place[0] + half_rows) & (row + PATCH > place[0])
    outer = (row < place[1] + HALO) & (row + PATCH > place[1])
    return inner | outer


def far_tile(place, phase, tiles):
    return jnp.where(place[3] == phase, tiles - 1, 0)


class Copies:
    def __init__(self, sems):
        self.sems, self.all = sems, []

    def start(self, source, target):
        copy = pltpu.make_async_copy(source, target, self.sems.at[len(self.all)])
        copy.start()
        self.all.append(copy)
        return copy

    def wait(self):
        for copy in self.all:
            copy.wait()


def staging_kernel(sides, _, core, *refs):
    col_refs, refs = refs[:sides], refs[sides:]
    cosine, sine, order, near, (ext, waves, *near_to), sems = *refs[:3], refs[3:7], refs[7:-1], refs[-1]
    for k, wave in enumerate((cosine, sine)):
        sorted_wave = sort_frequencies([wave[...]], order)
        for odd in range(2):
            waves[k, odd] = sorted_wave[:, odd * HALF : (odd + 1) * HALF]
    height, width = core.shape[1], core.shape[2]
    tiles = ext.shape[1]
    place = place_of(height)
    copies = Copies(sems)
    for t in range(width // LANE):
        part = core.at[:, :, pl.ds(t * LANE, LANE)]
        copies.start(part, ext.at[:, t + 1, pl.ds(HALO, height), :])
    for source, target in zip(near, near_to):
        copies.start(source, target)
    for j, ref in enumerate(col_refs):
        tile = far_tile(place, j, tiles)
        for p in range(2):
            for k, half in enumerate(unpacked(ref[p], place[3] != j)):
                ext[p + 2 * k, tile, HALO : HALO + height, :] = half
    copies.wait()


def patches_kernel(sides, cuts, peer, *refs):
    row_refs, refs = refs[: sides[0]], refs[sides[0] :]
    corner_refs, refs = refs[: sides[1]], refs[sides[1] :]
    own_info, peer_info, ext, own, probe, waves, tables, order = refs[:8]
    outs, (acc, queue, sems) = refs[9:-3], refs[-3:]
    tiles, height = ext.shape[1], ext.shape[2] - 2 * HALO
    half_rows = height // 2
    place = place_of(height)
    copies = Copies(sems)

    def far_row(phase):
        return pl.multiple_of(jnp.where(place[2] == phase, height + HALO, 0), 8)

    for i, ref in enumerate(row_refs):
        for t in range(tiles - 2):
            part = ref.at[:, :, pl.ds(t * LANE, LANE)]
            copies.start(part, ext.at[:, t + 1, pl.ds(far_row(i), HALO), :])
    for j, ref in enumerate(corner_refs):
        tile = far_tile(place, j, tiles)
        for i in range(sides[0]):
            rows = pl.ds(far_row(i), HALO)
            for p in range(2):
                for q, half in enumerate(unpacked(ref[i, p], place[3] != j)):
                    ext[p + 2 * q, tile, rows, :] = half
    first = pl.multiple_of(place[0] + HALO, 8)
    outer = pl.multiple_of(place[1] + HALO, 8)
    acc[:, :, pl.ds(first, half_rows), :] = jnp.zeros((4, tiles, half_rows, LANE), jnp.float32)
    acc[:, :, pl.ds(outer, HALO), :] = jnp.zeros((4, tiles, HALO, LANE), jnp.float32)

    def intensity(index):
        mine, theirs = jnp.minimum(index, PMAX - 1), jnp.maximum(index - PMAX, 0)
        return jnp.where(index < PMAX, own[mine], peer[theirs])

    copies.wait()
    length = jnp.int32(0)
    for index in range(2 * PMAX):
        info, slot = (own_info, index) if index < PMAX else (peer_info, index - PMAX)
        row, col, count = info[slot], info[PMAX + slot], info[2 * PMAX]
        queue[3 * length] = index
        queue[3 * length + 1] = row
        queue[3 * length + 2] = col
        length = length + ((slot < count) & wanted(place, row, half_rows)).astype(jnp.int32)

    def step(turn_at, carry):
        start = GROUP * turn_at
        items = [start] + [jnp.minimum(start + i, length - 1) for i in range(1, GROUP)]
        corners = [(queue[3 * i + 1], queue[3 * i + 2]) for i in items]
        ordered = sort_frequencies([intensity(queue[3 * i]) for i in items], order)
        rows = [ordered[i * PATCH : (i + 1) * PATCH] for i in range(GROUP)]
        intensities = [(x[:, :HALF], x[:, HALF:]) for x in rows]

        def put(i, slice_at, pair):
            if i == 0:
                deposit(acc, slice_at, *corners[i], pair)
            else:
                pl.when(start + i < length)(lambda: deposit(acc, slice_at, *corners[i], pair))

        patch_gradients(ext, corners, intensities, probe, waves, tables, put)
        return carry

    lax.fori_loop(0, (length + GROUP - 1) // GROUP, step, 0)
    gifts = Copies(sems)
    for target, parts in zip(outs, cuts):
        row_to = 0
        for tile, at, count in parts:
            tile = far_tile(place, tile[0], tiles) if isinstance(tile, tuple) else tile
            row = outer if at == OUTER else first
            row = row if at in (OUTER, None) else pl.multiple_of(first + place[at], 8)
            gifts.start(
                acc.at[:, pl.ds(tile, target.shape[1]), pl.ds(row, count), :],
                target.at[:, :, pl.ds(row_to, count), :],
            )
            row_to += count
    gifts.wait()


def near_tile(place, phase, tiles):
    return jnp.where(place[3] == phase, tiles - 1, 0)


def add_rims(place, out, rims, rim_row):
    _, tiles, rows, _ = out.shape
    for j, rim in enumerate(rims):
        at = near_tile(place, j, tiles)
        out[:, at, :, :] += rim[:, 0, pl.ds(rim_row, rows), :]


def edge_kernel(height, sides, open_left, open_right, outer_left, outer_right, *refs):
    place = place_of(height)
    rims, (open_out, outer_out) = refs[:sides], refs[-2:]
    open_out[:, 0:1] = open_left[...]
    open_out[:, 1:] = open_right[...]
    add_rims(place, open_out, rims, pl.multiple_of(place[5], 8))
    outer_out[:, 0:1] = outer_left[...]
    outer_out[:, 1:2] = outer_right[...]
    add_rims(place, outer_out, rims, height // 2)


def shut_inner_kernel(height, part, strip, out):
    place = place_of(height)
    out[...] = part[...]

    @pl.when(place[7] == 0)
    def _():
        out[...] += strip[...]


def shut_edge_kernel(height, sides, left, right, strip, *refs):
    place = place_of(height)
    rims, out = refs[:sides], refs[sides]
    out[:, 0:1] = left[...]
    out[:, 1:2] = right[...]
    add_rims(place, out, rims, pl.multiple_of(place[6], 8))

    @pl.when(place[7] == 0)
    def _():
        out[...] += strip[...]


def final_kernel(height, sides, part, *refs):
    place = place_of(height)
    shut_got, open_got, strip, rims = refs[:2], refs[2:4], refs[4:6], refs[6 : 6 + sides]
    out, work = refs[6 + sides :]
    work[...] = part[...]
    tiles = work.shape[1]
    add_rims(place, work, rims, pl.multiple_of(place[4], 8))

    def add(at, inner, edge):
        rows = pl.ds(pl.multiple_of(at, 8), inner.shape[2])
        split = 1 + inner.shape[1]
        work[:, 1:split, rows, :] += inner[...]
        work[:, 0:1, rows, :] += edge[:, 0:1]
        work[:, split:, rows, :] += edge[:, 1:]

    add(place[9], *open_got)
    add(place[8], *shut_got)

    @pl.when(place[7] == 1)
    def _():
        add(place[8], *strip)

    for t in range(tiles):
        out[:, :, t * LANE : (t + 1) * LANE] = work[:, t]


def half_kernel(height, sides, part, inner, edge, *refs):
    place = place_of(height)
    rims, out = refs[:sides], refs[sides]
    out[...] = part[...]
    add_rims(place, out, rims, 0)
    tiles = out.shape[1]
    rows = pl.ds(pl.multiple_of(jnp.where(place[0] == 0, 0, out.shape[2] - HALO), 8), HALO)
    out[:, 1 : tiles - 1, rows, :] += inner[...]
    out[:, 0:1, rows, :] += edge[:, 0:1]
    out[:, tiles - 1 : tiles, rows, :] += edge[:, 1:2]


def near_rows(place, phase, height):
    return pl.ds(pl.multiple_of(jnp.where(place[2] == phase, height - HALO, 0), HALO), HALO)


def near_cols(place, phase, width):
    return pl.ds(pl.multiple_of(jnp.where(place[3] == phase, width - LANE, 0), LANE), LANE)


def sort_frequencies(arrays, order):
    values = side(arrays, 1)
    total = None
    for _ in range(3):
        part = values.astype(jnp.bfloat16)
        values = values - part.astype(jnp.float32)
        rows = times(order[1], part)
        rows = side([rows[:, i * PATCH : (i + 1) * PATCH] for i in range(len(arrays))], 0)
        moved = times(rows, order[0])
        total = moved if total is None else total + moved
    return total


def packed(strips, high):
    low_lanes = lax.broadcasted_iota(jnp.int32, strips[0].shape, 1) < HALO
    turns = [jnp.where(high, LANE - HALO, 0), jnp.where(high, 0, HALO)]
    parts = [pltpu.roll(strip, turn, 1) for strip, turn in zip(strips, turns)]
    return jnp.where(low_lanes, *parts)


def unpacked(tile, high):
    return [
        pltpu.roll(tile, turn, 1)
        for turn in (jnp.where(high, HALO, 0), jnp.where(high, 0, LANE - HALO))
    ]


def edges_kernel(sides, core, *refs):
    outs, (cols, sems) = refs[:-2], refs[-2:]
    copies = Copies(sems)
    height, width = core.shape[1:]
    place = place_of(height)
    for j in range(sides[1]):
        copies.start(core.at[:, :, near_cols(place, j, width)], cols.at[j])
    for i in range(sides[0]):
        copies.start(core.at[:, near_rows(place, i, height), :], outs[i])
    copies.wait()
    for j in range(sides[1]):
        high = place[3] == j
        for p in range(2):
            outs[sides[0] + j][p] = packed([cols[j, p], cols[j, p + 2]], high)


def corners_kernel(sides, _, *refs):
    strips, outs = refs[: sides[0]], refs[sides[0] :]
    width = strips[0].shape[2]
    for j, out in enumerate(outs):
        high = lax.axis_index("col") % 2 == j
        cols = pl.ds(pl.multiple_of(jnp.where(high, width - LANE, 0), LANE), LANE)
        for i, strip in enumerate(strips):
            for p in range(2):
                out[i, p] = packed([strip[p, :, cols], strip[p + 2, :, cols]], high)


ANY = pl.BlockSpec(memory_space=pl.ANY)
VMEM = pl.BlockSpec(memory_space=pltpu.VMEM)
SMEM = pl.BlockSpec(memory_space=pltpu.SMEM)


def block(*shape):
    return jax.ShapeDtypeStruct(shape, jnp.float32)


def call(kernel, out_shapes, in_specs, out_specs, scratch, *operands, limit=VMEM_LIMIT, aliases=None):
    return pl.pallas_call(
        kernel,
        out_shape=out_shapes,
        in_specs=in_specs,
        out_specs=out_specs,
        scratch_shapes=scratch,
        input_output_aliases=aliases or {},
        compiler_params=pltpu.CompilerParams(vmem_limit_bytes=limit),
        cost_estimate=pl.CostEstimate(flops=0, bytes_accessed=0, transcendentals=0),
    )(*operands)


def shards(object_field, probe_field, prop_phase, measured, positions, counts):
    height, width = object_field.shape[2:]
    shard_count = lax.axis_size("scan")
    half_rows = height // 2
    band = height // shard_count
    rest = band - HALO
    tiles = width // LANE
    row_sides = pairings(lax.axis_size("row"))
    col_sides = pairings(lax.axis_size("col"))
    sides = len(col_sides)
    both = (len(row_sides), sides)
    stride = shard_count // 2
    scan_at = lax.axis_index("scan")
    planes = object_field.reshape(4, height, width)
    own = measured.reshape(PMAX, PATCH, PATCH)
    order = sorted_columns()
    own_info = jnp.concatenate(
        [positions.reshape(PMAX, 2).T.reshape(-1), counts.reshape(1), jnp.zeros((1,), jnp.int32)]
    ).astype(jnp.int32)

    def across(value):
        return lax.ppermute(value, "scan", [(i, i ^ stride) for i in range(shard_count)])

    def to_cols(value, j):
        return joint_permute(value, ("col",), lambda c: (pair_of(c, j),))

    def to_rows(value, i):
        return joint_permute(value, ("row",), lambda r: (pair_of(r, i),))

    peer = across(own)
    peer_info = across(own_info)
    edge_shapes = (
        [block(4, HALO, width)] * both[0]
        + [block(2, height, LANE)] * sides
    )
    edges = call(
        functools.partial(edges_kernel, both),
        edge_shapes,
        [ANY],
        [VMEM] * len(edge_shapes),
        [pltpu.VMEM((sides, 4, height, LANE), jnp.float32), pltpu.SemaphoreType.DMA((sum(both),))],
        planes,
        limit=VMEM_LITTLE,
    )
    row_halos = [to_rows(edges[i], i) for i in row_sides]
    col_halos = [to_cols(edges[both[0] + j], j) for j in col_sides]
    cosine, sine = jnp.cos(prop_phase), jnp.sin(prop_phase)
    tables = block_tables()

    two_bands = shard_count == 4 and rest > 0
    inner = tiles - 2
    cuts = [(inner, [(2, OUTER, HALO)]), (1, [(1, OUTER, HALO)]), (1, [(tiles, OUTER, HALO)])]
    cuts += [(1, [((j,), None, half_rows), ((j,), OUTER, HALO)]) for j in col_sides]
    if two_bands:
        early = inner
        right = tiles - early - 1
        cuts += [(early, [(2, 5, rest)]), (1, [(1, 5, rest)]), (right, [(2 + early, 5, rest)])]
        cuts += [(inner, [(2, 6, HALO)]), (1, [(1, 6, HALO)]), (1, [(tiles, 6, HALO)])]
        cuts += [(tiles, [(1, 4, band)])]
    else:
        cuts += [(tiles, [(1, None, half_rows)]), (1, [(1, None, HALO)]), (1, [(1, None, HALO)])]
    full = (4, tiles + 2, height + 2 * HALO, LANE)
    ext, waves, lamp, near_tables, near_own, near_order = call(
        functools.partial(staging_kernel, sides),
        [
            block(*full),
            block(2, 2, PATCH, HALF),
            block(*probe_field.shape),
            jax.ShapeDtypeStruct(tables.shape, tables.dtype),
            block(*own.shape),
            jax.ShapeDtypeStruct(order.shape, order.dtype),
        ],
        [SMEM, ANY] + [VMEM] * (sides + 3) + [ANY] * 4,
        [VMEM] * 6,
        [pltpu.SemaphoreType.DMA((tiles + 4,))],
        own_info,
        planes,
        *col_halos,
        cosine,
        sine,
        order,
        probe_field,
        tables,
        own,
        order,
        limit=VMEM_LITTLE,
    )
    row_ends = call(
        functools.partial(corners_kernel, both),
        [block(both[0], 2, HALO, LANE)] * sides,
        [VMEM] * (1 + both[0]),
        [VMEM] * sides,
        [],
        near_order,
        *row_halos,
        limit=VMEM_LITTLE,
    )
    corner_halos = [to_cols(ends, j) for j, ends in zip(col_sides, row_ends)]
    arrivals = [peer, *row_halos, *corner_halos]
    copy_count = max(
        tiles * both[0], sum(len(parts) for _, parts in cuts)
    )
    outs = call(
        functools.partial(patches_kernel, both, [parts for _, parts in cuts]),
        [block(*full)] + [block(4, wide, sum(part[2] for part in parts), LANE) for wide, parts in cuts],
        [VMEM] + [ANY] * both[0] + [VMEM] * sides + [SMEM, SMEM] + [VMEM] * 6,
        [VMEM] + [ANY] * len(cuts),
        [
            pltpu.VMEM(full, jnp.float32),
            pltpu.SMEM((3 * (2 * PMAX + 1),), jnp.int32),
            pltpu.SemaphoreType.DMA((copy_count,)),
        ],
        *arrivals,
        own_info,
        peer_info,
        ext,
        near_own,
        lamp,
        waves,
        near_tables,
        near_order,
        aliases={len(arrivals) + 2: 0},
    )[1:]
    outer_inner, outer_left, outer_right = outs[:3]
    rims, pieces = outs[3 : 3 + sides], outs[3 + sides :]

    def to_next(value):
        return joint_permute(
            value, ("row", "scan"), lambda r, s: (r + 1 if s < stride else r - 1, s)
        )

    def beside(value, mask=1):
        return lax.ppermute(value, "scan", [(i, i ^ mask) for i in range(shard_count)])

    def fold(kernel, out_shapes, *operands, scratch=()):
        many = isinstance(out_shapes, tuple)
        return call(
            functools.partial(kernel, height),
            out_shapes,
            [VMEM] * len(operands),
            (VMEM,) * len(out_shapes) if many else VMEM,
            list(scratch),
            *operands,
            limit=VMEM_LITTLE,
        )

    got_rims = [to_cols(rim, j) for j, rim in zip(col_sides, rims)]
    got_inner = to_next(outer_inner)
    open_edge, outer_edge = fold(
        lambda *refs: edge_kernel(refs[0], sides, *refs[1:]),
        (
            block(4, 1 + pieces[2].shape[1], pieces[1].shape[2], LANE),
            block(4, 2, HALO, LANE),
        ),
        pieces[1],
        pieces[2],
        outer_left,
        outer_right,
        *got_rims,
    )
    got_edge = to_next(outer_edge)
    if not two_bands:
        half = fold(
            lambda *refs: half_kernel(refs[0], sides, *refs[1:]),
            block(4, tiles, half_rows, LANE),
            pieces[0],
            got_inner,
            got_edge,
            *got_rims,
        )
        mask = stride // 2
        while mask > 0:
            size = half.shape[2] // 2
            low = (scan_at & mask) == 0
            keep = lax.dynamic_slice_in_dim(half, jnp.where(low, 0, size), size, axis=2)
            send = lax.dynamic_slice_in_dim(half, jnp.where(low, size, 0), size, axis=2)
            half = keep + beside(send, mask)
            mask //= 2
        return half.transpose(0, 2, 1, 3).reshape(2, 2, band, width)
    got_open = [beside(pieces[0]), beside(open_edge)]
    got_open[0], got_inner = lax.optimization_barrier((got_open[0], got_inner))
    got_open[1], got_edge = lax.optimization_barrier((got_open[1], got_edge))
    shut_inner = fold(shut_inner_kernel, block(4, inner, HALO, LANE), pieces[3], got_inner)
    got_shut = [beside(shut_inner)]
    shut_edge = fold(
        lambda *refs: shut_edge_kernel(refs[0], sides, *refs[1:]),
        block(4, 2, HALO, LANE),
        pieces[4],
        pieces[5],
        got_edge,
        *got_rims,
    )
    got_shut.append(beside(shut_edge))
    total = fold(
        lambda *refs: final_kernel(refs[0], sides, *refs[1:]),
        block(4, band, width),
        pieces[6],
        *got_shut,
        *got_open,
        got_inner,
        got_edge,
        *got_rims,
        scratch=[pltpu.VMEM((4, tiles, band, LANE), jnp.float32)],
    )
    return total.reshape(2, 2, band, width)


def solution(mesh):
    placed = (
        P(None, None, "row", "col"),
        P(),
        P(),
        P("row", "col", "scan", None, None, None),
        P("row", "col", "scan", None, None),
        P("row", "col", "scan"),
    )
    return jax.shard_map(
        shards,
        mesh=mesh,
        in_specs=placed,
        out_specs=P(None, None, ("row", "scan"), "col"),
        check_vma=False,
    )
```

```python
import functools
import math

import jax
import jax.numpy as jnp
import numpy as np
from jax import lax
from jax.experimental import pallas as pl
from jax.experimental.pallas import tpu as pltpu
from jax.sharding import PartitionSpec as P

PATCH = 256
HALO = 64
PMAX = 3
LANE = 128
HALF = PATCH // 2
VMEM_LIMIT = 32 * 1024 * 1024
VMEM_LITTLE = 8 * 1024 * 1024
GROUP = 4
ROWS = 16


def block_tables():
    index = np.arange(HALF)
    tables = []
    for odd in range(2):
        angles = ((2 * index[:, None] + odd) * index[None, :] % PATCH) * (2.0 * math.pi / PATCH)
        cosines = np.cos(angles) / math.sqrt(PATCH)
        sines = np.sin(angles) / math.sqrt(PATCH)
        tables.append(np.block([[cosines, sines], [-sines, cosines]]))
    tables += [table.T for table in tables]
    return jnp.asarray(np.stack(tables).astype(np.float32)).astype(jnp.bfloat16)


def sorted_columns():
    index = np.arange(PATCH)
    matrix = np.zeros((PATCH, PATCH), np.float32)
    matrix[index, index % 2 * HALF + index // 2] = 1.0
    return jnp.asarray(np.stack([matrix, matrix.T])).astype(jnp.bfloat16)


def pair_of(index, phase):
    return index + 1 if index % 2 == phase else index - 1


def pairings(size):
    return range(1 if size <= 2 else 2)


def joint_permute(value, names, targets):
    sizes = [lax.axis_size(name) for name in names]
    route = []
    for flat in range(math.prod(sizes)):
        place = np.unravel_index(flat, sizes)
        goal = targets(*[int(i) for i in place])
        if goal is None or any(not 0 <= g < s for g, s in zip(goal, sizes)):
            continue
        route.append((flat, int(np.ravel_multi_index(goal, sizes))))
    return lax.ppermute(value, tuple(names) if len(names) > 1 else names[0], route)


OUTER = -1


def times(a, b):
    return jnp.dot(a, b, preferred_element_type=jnp.float32)


def side(parts, axis):
    return jnp.concatenate(parts, axis=axis)


def product(a, b):
    return a[0] * b[0] - a[1] * b[1], a[0] * b[1] + a[1] * b[0]


def conj_product(a, b):
    return a[0] * b[0] + a[1] * b[1], a[0] * b[1] - a[1] * b[0]


def by_lanes(multiply, a, b):
    pairs = [multiply([x[k] for x in a], [x[k] for x in b]) for k in range(2)]
    return [[pair[part] for pair in pairs] for part in range(2)]


def at_rows(start, count=ROWS):
    return slice(start, start + count)


def at_lanes(tile):
    return slice(tile * LANE, (tile + 1) * LANE)


def corner_of(row, col):
    return row + HALO, (col + LANE) // LANE, lax.rem(col + LANE, LANE)


class Patches:
    def __init__(self, x, y, p, z, near, far, tables):
        self.x, self.y, self.p, self.z, self.tables = x, y, p, z, tables
        self.near, self.far, self.count = near, far, near.shape[0]
        self.lane = lax.broadcasted_iota(jnp.int32, (ROWS, LANE), 1)

    def window(self, ext, slice_at, corner, start):
        top, tile, shift = corner_of(*corner)
        turn, inside = lax.rem(LANE - shift, LANE), self.lane < LANE - shift
        rows = pl.ds(top + start, ROWS)
        parts = []
        for plane in (2 * slice_at, 2 * slice_at + 1):
            moved = [pltpu.roll(ext[plane, tile + j, rows, :], turn, 1) for j in range(3)]
            parts.append([jnp.where(inside, moved[j], moved[j + 1]) for j in range(2)])
        return parts

    def deposit(self, acc, slice_at, corner, start, block, live):
        top, tile, shift = corner_of(*corner)
        inside, rows = self.lane >= shift, pl.ds(top + start, ROWS)
        for part in range(2):
            moved = [pltpu.roll(jnp.where(live, b, 0.0), shift, 1) for b in block[part]]
            sums = [
                jnp.where(inside, moved[0], 0.0),
                jnp.where(inside, moved[1], moved[0]),
                jnp.where(inside, 0.0, moved[1]),
            ]
            for j in range(3):
                acc[2 * slice_at + part, tile + j, rows, :] += sums[j]

    def fill(self, i, row, blocks):
        for part in range(2):
            for k in range(2):
                low, high = blocks[0][part][k], blocks[1][part][k]
                rows, lanes = at_rows(part * HALF + row), at_lanes(2 * i + k)
                self.x[0, rows, lanes] = (low + high).astype(jnp.bfloat16)
                self.x[1, rows, lanes] = (low - high).astype(jnp.bfloat16)

    def multiply_left(self, *tables):
        for odd, table in enumerate(tables):
            for i in range(self.count):
                part = slice(i * PATCH, (i + 1) * PATCH)
                self.y[odd, :, part] = times(table, self.x[odd, :, part])
            yield

    def multiply_right(self, *tables):
        for odd, table in enumerate(tables):
            self.z[odd] = times(self.p[odd], table)
            yield

    def to_frequencies(self):
        yield from self.multiply_left(self.tables[0], self.tables[1])
        for i in range(self.count):
            for a in range(2):
                for row in range(0, HALF, ROWS):
                    for part in range(2):
                        rows = at_rows(part * HALF + row)
                        low, high = [self.y[a, rows, at_lanes(2 * i + k)] for k in range(2)]
                        rows = at_rows((2 * i + a) * HALF + row)
                        self.p[0, rows, at_lanes(part)] = (low + high).astype(jnp.bfloat16)
                        self.p[1, rows, at_lanes(part)] = (low - high).astype(jnp.bfloat16)
            yield
        yield from self.multiply_right(self.tables[2], self.tables[3])

    def change(self, function):
        for i in range(self.count):
            for a in range(2):
                for row in range(0, HALF, ROWS):
                    rows = at_rows((2 * i + a) * HALF + row)
                    for b in range(2):
                        value = [self.z[b, rows, at_lanes(part)] for part in range(2)]
                        result = function(i, b, a * HALF + row, value)
                        for part in range(2):
                            to = at_rows(part * HALF + row)
                            self.x[a, to, at_lanes(2 * i + b)] = result[part].astype(jnp.bfloat16)
            yield

    def from_frequencies(self):
        yield from self.multiply_left(self.tables[2], self.tables[3])
        for i in range(self.count):
            for b in range(2):
                for row in range(0, HALF, ROWS):
                    for part in range(2):
                        rows = at_rows(part * HALF + row)
                        even, odd = [self.y[a, rows, at_lanes(2 * i + b)] for a in range(2)]
                        rows = [at_rows((2 * i + half) * HALF + row) for half in range(2)]
                        self.p[b, rows[0], at_lanes(part)] = (even + odd).astype(jnp.bfloat16)
                        self.p[b, rows[1], at_lanes(part)] = (even - odd).astype(jnp.bfloat16)
            yield
        yield from self.multiply_right(self.tables[0], self.tables[1])

    def result(self, i, half, row):
        rows, parts = at_rows((2 * i + half) * HALF + row), []
        for part in range(2):
            even, odd = [self.z[b, rows, at_lanes(part)] for b in range(2)]
            parts.append([even + odd, even - odd])
        return parts

    def last(self, row):
        return row + ROWS == HALF

    def blocks(self):
        return [(i, row) for i in range(self.count) for row in range(0, HALF, ROWS)]


def block_of(ref, i, half, row):
    rows = at_rows(half * HALF + row)
    return [[ref[i, part, rows, at_lanes(k)] for k in range(2)] for part in range(2)]


def keep_block(ref, i, half, row, block):
    rows = at_rows(half * HALF + row)
    for part in range(2):
        for k in range(2):
            ref[i, part, rows, at_lanes(k)] = block[part][k]


def patch_gradients(patches, ext, acc, corners, lives, intensity, probe, waves):
    near, far = patches.near, patches.far

    def lamp(half, row):
        rows = at_rows(half * HALF + row)
        return [[probe[part, rows, at_lanes(k)] for k in range(2)] for part in range(2)]

    def prop(b, row):
        return [waves[part, b, at_rows(row), :] for part in range(2)]

    for i, row in patches.blocks():
        patches.fill(
            i,
            row,
            [
                by_lanes(
                    product, lamp(half, row), patches.window(ext, 0, corners[i], half * HALF + row)
                )
                for half in range(2)
            ],
        )
        if patches.last(row):
            yield
    yield from patches.to_frequencies()
    yield from patches.change(lambda i, b, row, z: product(prop(b, row), z))
    yield from patches.from_frequencies()
    for i, row in patches.blocks():
        leaving = []
        for half in range(2):
            arrived = patches.result(i, half, row)
            second = patches.window(ext, 1, corners[i], half * HALF + row)
            keep_block(near, i, half, row, arrived)
            keep_block(far, i, half, row, second)
            leaving.append(by_lanes(product, second, arrived))
        patches.fill(i, row, leaving)
        if patches.last(row):
            yield
    yield from patches.to_frequencies()

    def residual(i, b, row, z):
        misfit = z[0] * z[0] + z[1] * z[1] - intensity[at_rows(i * PATCH + row), at_lanes(b)]
        return misfit * z[0], misfit * z[1]

    yield from patches.change(residual)
    yield from patches.from_frequencies()
    for i, row in patches.blocks():
        through = []
        for half in range(2):
            back = patches.result(i, half, row)
            start = half * HALF + row
            grad = by_lanes(conj_product, block_of(near, i, half, row), back)
            patches.deposit(acc, 1, corners[i], start, grad, lives[i])
            through.append(by_lanes(conj_product, block_of(far, i, half, row), back))
        patches.fill(i, row, through)
        if patches.last(row):
            yield
    yield from patches.to_frequencies()
    yield from patches.change(lambda i, b, row, z: conj_product(prop(b, row), z))
    yield from patches.from_frequencies()
    for i, row in patches.blocks():
        for half in range(2):
            grad = by_lanes(conj_product, lamp(half, row), patches.result(i, half, row))
            patches.deposit(acc, 0, corners[i], half * HALF + row, grad, lives[i])
        if patches.last(row):
            yield


def in_turns(first, second):
    for _ in range(GROUP // 2):
        next(first)
    going = [first, second]
    while going:
        for group in list(going):
            try:
                next(group)
            except StopIteration:
                going.remove(group)


def place_of(height):
    shard_count = lax.axis_size("scan")
    scan_at = lax.axis_index("scan")
    band = height // shard_count
    upper = scan_at < shard_count // 2
    even = scan_at % 2 == 0
    open_at = jnp.where(upper, HALO, 0)
    shut_at = jnp.where(upper, 0, band - HALO)
    other_at = jnp.where(even, band, 0)
    return [
        jnp.where(upper, 0, height // 2),
        jnp.where(upper, height, -HALO),
        lax.axis_index("row") % 2,
        lax.axis_index("col") % 2,
        jnp.where(even, 0, band),
        other_at + open_at,
        other_at + shut_at,
        ((scan_at == 0) | (scan_at == shard_count - 1)).astype(jnp.int32),
        shut_at,
        open_at,
    ]


def wanted(place, row, half_rows):
    inner = (row < place[0] + half_rows) & (row + PATCH > place[0])
    outer = (row < place[1] + HALO) & (row + PATCH > place[1])
    return inner | outer


def far_tile(place, phase, tiles):
    return jnp.where(place[3] == phase, tiles - 1, 0)


class Copies:
    def __init__(self, sems):
        self.sems, self.all = sems, []

    def start(self, source, target):
        copy = pltpu.make_async_copy(source, target, self.sems.at[len(self.all)])
        copy.start()
        self.all.append(copy)
        return copy

    def wait(self):
        for copy in self.all:
            copy.wait()


def staging_kernel(sides, _, core, *refs):
    col_refs, refs = refs[:sides], refs[sides:]
    cosine, sine, order, near, (ext, waves, *near_to), sems = *refs[:3], refs[3:7], refs[7:-1], refs[-1]
    for k, wave in enumerate((cosine, sine)):
        sorted_wave = sort_frequencies([wave[...]], order)
        for odd in range(2):
            waves[k, odd] = sorted_wave[:, odd * HALF : (odd + 1) * HALF]
    height, width = core.shape[1], core.shape[2]
    tiles = ext.shape[1]
    place = place_of(height)
    copies = Copies(sems)
    for t in range(width // LANE):
        part = core.at[:, :, pl.ds(t * LANE, LANE)]
        copies.start(part, ext.at[:, t + 1, pl.ds(HALO, height), :])
    for source, target in zip(near, near_to):
        copies.start(source, target)
    for j, ref in enumerate(col_refs):
        tile = far_tile(place, j, tiles)
        for p in range(2):
            for k, half in enumerate(unpacked(ref[p], place[3] != j)):
                ext[p + 2 * k, tile, HALO : HALO + height, :] = half
    copies.wait()


def patches_kernel(sides, cuts, peer, *refs):
    row_refs, refs = refs[: sides[0]], refs[sides[0] :]
    corner_refs, refs = refs[: sides[1]], refs[sides[1] :]
    own_info, peer_info, ext, own, probe, waves, tables, order = refs[:8]
    outs, (acc, queue, *scratch, ordered, sems) = refs[9:-16], refs[-16:]
    groups = [Patches(*scratch[:6], tables), Patches(*scratch[6:], tables)]
    tiles, height = ext.shape[1], ext.shape[2] - 2 * HALO
    half_rows = height // 2
    place = place_of(height)
    copies = Copies(sems)

    def far_row(phase):
        return pl.multiple_of(jnp.where(place[2] == phase, height + HALO, 0), 8)

    for i, ref in enumerate(row_refs):
        for t in range(tiles - 2):
            part = ref.at[:, :, pl.ds(t * LANE, LANE)]
            copies.start(part, ext.at[:, t + 1, pl.ds(far_row(i), HALO), :])
    for j, ref in enumerate(corner_refs):
        tile = far_tile(place, j, tiles)
        for i in range(sides[0]):
            rows = pl.ds(far_row(i), HALO)
            for p in range(2):
                for q, half in enumerate(unpacked(ref[i, p], place[3] != j)):
                    ext[p + 2 * q, tile, rows, :] = half
    first = pl.multiple_of(place[0] + HALO, 8)
    outer = pl.multiple_of(place[1] + HALO, 8)
    acc[:, :, pl.ds(first, half_rows), :] = jnp.zeros((4, tiles, half_rows, LANE), jnp.float32)
    acc[:, :, pl.ds(outer, HALO), :] = jnp.zeros((4, tiles, HALO, LANE), jnp.float32)

    def intensity(index):
        mine, theirs = jnp.minimum(index, PMAX - 1), jnp.maximum(index - PMAX, 0)
        return jnp.where(index < PMAX, own[mine], peer[theirs])

    copies.wait()
    length = jnp.int32(0)
    for index in range(2 * PMAX):
        info, slot = (own_info, index) if index < PMAX else (peer_info, index - PMAX)
        row, col, count = info[slot], info[PMAX + slot], info[2 * PMAX]
        queue[3 * length] = index
        queue[3 * length + 1] = row
        queue[3 * length + 2] = col
        length = length + ((slot < count) & wanted(place, row, half_rows)).astype(jnp.int32)

    def step(turn_at, carry):
        start = GROUP * turn_at
        items = [start] + [jnp.minimum(start + i, length - 1) for i in range(1, GROUP)]
        corners = [(queue[3 * i + 1], queue[3 * i + 2]) for i in items]
        lives = [start + i < length for i in range(GROUP)]
        ordered[...] = sort_frequencies([intensity(queue[3 * i]) for i in items], order)
        steps = []
        for k, patches in enumerate(groups):
            part = slice(k * patches.count, (k + 1) * patches.count)
            intensities = ordered.at[pl.ds(k * patches.count * PATCH, patches.count * PATCH)]
            steps.append(
                patch_gradients(
                    patches, ext, acc, corners[part], lives[part], intensities, probe, waves
                )
            )
        in_turns(*steps)
        return carry

    lax.fori_loop(0, (length + GROUP - 1) // GROUP, step, 0)
    gifts = Copies(sems)
    for target, parts in zip(outs, cuts):
        row_to = 0
        for tile, at, count in parts:
            tile = far_tile(place, tile[0], tiles) if isinstance(tile, tuple) else tile
            row = outer if at == OUTER else first
            row = row if at in (OUTER, None) else pl.multiple_of(first + place[at], 8)
            gifts.start(
                acc.at[:, pl.ds(tile, target.shape[1]), pl.ds(row, count), :],
                target.at[:, :, pl.ds(row_to, count), :],
            )
            row_to += count
    gifts.wait()


def near_tile(place, phase, tiles):
    return jnp.where(place[3] == phase, tiles - 1, 0)


def add_rims(place, out, rims, rim_row):
    _, tiles, rows, _ = out.shape
    for j, rim in enumerate(rims):
        at = near_tile(place, j, tiles)
        out[:, at, :, :] += rim[:, 0, pl.ds(rim_row, rows), :]


def edge_kernel(height, sides, open_left, open_right, outer_left, outer_right, *refs):
    place = place_of(height)
    rims, (open_out, outer_out) = refs[:sides], refs[-2:]
    open_out[:, 0:1] = open_left[...]
    open_out[:, 1:] = open_right[...]
    add_rims(place, open_out, rims, pl.multiple_of(place[5], 8))
    outer_out[:, 0:1] = outer_left[...]
    outer_out[:, 1:2] = outer_right[...]
    add_rims(place, outer_out, rims, height // 2)


def shut_inner_kernel(height, part, strip, out):
    place = place_of(height)
    out[...] = part[...]

    @pl.when(place[7] == 0)
    def _():
        out[...] += strip[...]


def shut_edge_kernel(height, sides, left, right, strip, *refs):
    place = place_of(height)
    rims, out = refs[:sides], refs[sides]
    out[:, 0:1] = left[...]
    out[:, 1:2] = right[...]
    add_rims(place, out, rims, pl.multiple_of(place[6], 8))

    @pl.when(place[7] == 0)
    def _():
        out[...] += strip[...]


def gather_kernel(height, sides, part, *refs):
    place = place_of(height)
    shut_got, open_got, strip, rims = refs[0], refs[1:3], refs[3:5], refs[5 : 5 + sides]
    out, edge_out, work = refs[5 + sides :]
    work[...] = part[...]
    tiles = work.shape[1]
    add_rims(place, work, rims, pl.multiple_of(place[4], 8))

    def add(at, inner, edge=None):
        rows = pl.ds(pl.multiple_of(at, 8), inner.shape[2])
        split = 1 + inner.shape[1]
        work[:, 1:split, rows, :] += inner[...]
        if edge is not None:
            work[:, 0:1, rows, :] += edge[:, 0:1]
            work[:, split:, rows, :] += edge[:, 1:]

    add(place[9], *open_got)
    add(place[8], shut_got)

    @pl.when(place[7] == 1)
    def _():
        add(place[8], *strip)

    shut_rows = pl.ds(pl.multiple_of(place[8], 8), HALO)
    edge_out[:, 0:1] = work[:, 0:1, shut_rows, :]
    edge_out[:, 1:2] = work[:, tiles - 1 :, shut_rows, :]
    for t in range(tiles):
        out[:, :, t * LANE : (t + 1) * LANE] = work[:, t]


def last_kernel(height, total, edge, got, out, work, sems):
    place = place_of(height)
    rows = pl.ds(pl.multiple_of(place[8], 8), HALO)
    work[...] = edge[...] + got[...]
    copies = Copies(sems)
    for k in range(2):
        lanes = pl.ds(k * (out.shape[2] - LANE), LANE)
        copies.start(work.at[:, k], out.at[:, rows, lanes])
    copies.wait()


def half_kernel(height, sides, part, inner, edge, *refs):
    place = place_of(height)
    rims, out = refs[:sides], refs[sides]
    out[...] = part[...]
    add_rims(place, out, rims, 0)
    tiles = out.shape[1]
    rows = pl.ds(pl.multiple_of(jnp.where(place[0] == 0, 0, out.shape[2] - HALO), 8), HALO)
    out[:, 1 : tiles - 1, rows, :] += inner[...]
    out[:, 0:1, rows, :] += edge[:, 0:1]
    out[:, tiles - 1 : tiles, rows, :] += edge[:, 1:2]


def near_rows(place, phase, height):
    return pl.ds(pl.multiple_of(jnp.where(place[2] == phase, height - HALO, 0), HALO), HALO)


def near_cols(place, phase, width):
    return pl.ds(pl.multiple_of(jnp.where(place[3] == phase, width - LANE, 0), LANE), LANE)


def sort_frequencies(arrays, order):
    values = side(arrays, 1)
    total = None
    for _ in range(3):
        part = values.astype(jnp.bfloat16)
        values = values - part.astype(jnp.float32)
        rows = times(order[1], part).astype(jnp.bfloat16)
        rows = side([rows[:, i * PATCH : (i + 1) * PATCH] for i in range(len(arrays))], 0)
        moved = times(rows, order[0])
        total = moved if total is None else total + moved
    return total


def packed(strips, high):
    low_lanes = lax.broadcasted_iota(jnp.int32, strips[0].shape, 1) < HALO
    turns = [jnp.where(high, LANE - HALO, 0), jnp.where(high, 0, HALO)]
    parts = [pltpu.roll(strip, turn, 1) for strip, turn in zip(strips, turns)]
    return jnp.where(low_lanes, *parts)


def unpacked(tile, high):
    return [
        pltpu.roll(tile, turn, 1)
        for turn in (jnp.where(high, HALO, 0), jnp.where(high, 0, LANE - HALO))
    ]


def edges_kernel(sides, core, *refs):
    outs, (cols, sems) = refs[:-2], refs[-2:]
    copies = Copies(sems)
    height, width = core.shape[1:]
    place = place_of(height)
    for j in range(sides[1]):
        copies.start(core.at[:, :, near_cols(place, j, width)], cols.at[j])
    for i in range(sides[0]):
        copies.start(core.at[:, near_rows(place, i, height), :], outs[i])
    copies.wait()
    for j in range(sides[1]):
        high = place[3] == j
        for p in range(2):
            outs[sides[0] + j][p] = packed([cols[j, p], cols[j, p + 2]], high)


def corners_kernel(sides, _, *refs):
    strips, outs = refs[: sides[0]], refs[sides[0] :]
    width = strips[0].shape[2]
    for j, out in enumerate(outs):
        high = lax.axis_index("col") % 2 == j
        cols = pl.ds(pl.multiple_of(jnp.where(high, width - LANE, 0), LANE), LANE)
        for i, strip in enumerate(strips):
            for p in range(2):
                out[i, p] = packed([strip[p, :, cols], strip[p + 2, :, cols]], high)


ANY = pl.BlockSpec(memory_space=pl.ANY)
VMEM = pl.BlockSpec(memory_space=pltpu.VMEM)
SMEM = pl.BlockSpec(memory_space=pltpu.SMEM)


def block(*shape):
    return jax.ShapeDtypeStruct(shape, jnp.float32)


def call(kernel, out_shapes, in_specs, out_specs, scratch, *operands, limit=VMEM_LIMIT, aliases=None):
    return pl.pallas_call(
        kernel,
        out_shape=out_shapes,
        in_specs=in_specs,
        out_specs=out_specs,
        scratch_shapes=scratch,
        input_output_aliases=aliases or {},
        compiler_params=pltpu.CompilerParams(vmem_limit_bytes=limit),
        cost_estimate=pl.CostEstimate(flops=0, bytes_accessed=0, transcendentals=0),
    )(*operands)


def shards(object_field, probe_field, prop_phase, measured, positions, counts):
    height, width = object_field.shape[2:]
    shard_count = lax.axis_size("scan")
    half_rows = height // 2
    band = height // shard_count
    rest = band - HALO
    tiles = width // LANE
    row_sides = pairings(lax.axis_size("row"))
    col_sides = pairings(lax.axis_size("col"))
    sides = len(col_sides)
    both = (len(row_sides), sides)
    stride = shard_count // 2
    scan_at = lax.axis_index("scan")
    planes = object_field.reshape(4, height, width)
    own = measured.reshape(PMAX, PATCH, PATCH)
    order = sorted_columns()
    own_info = jnp.concatenate(
        [positions.reshape(PMAX, 2).T.reshape(-1), counts.reshape(1), jnp.zeros((1,), jnp.int32)]
    ).astype(jnp.int32)

    def across(value):
        return lax.ppermute(value, "scan", [(i, i ^ stride) for i in range(shard_count)])

    def to_cols(value, j):
        return joint_permute(value, ("col",), lambda c: (pair_of(c, j),))

    def to_rows(value, i):
        return joint_permute(value, ("row",), lambda r: (pair_of(r, i),))

    peer = across(own)
    peer_info = across(own_info)
    edge_shapes = (
        [block(4, HALO, width)] * both[0]
        + [block(2, height, LANE)] * sides
    )
    edges = call(
        functools.partial(edges_kernel, both),
        edge_shapes,
        [ANY],
        [VMEM] * len(edge_shapes),
        [pltpu.VMEM((sides, 4, height, LANE), jnp.float32), pltpu.SemaphoreType.DMA((sum(both),))],
        planes,
        limit=VMEM_LITTLE,
    )
    row_halos = [to_rows(edges[i], i) for i in row_sides]
    col_halos = [to_cols(edges[both[0] + j], j) for j in col_sides]
    cosine, sine = jnp.cos(prop_phase), jnp.sin(prop_phase)
    tables = block_tables()

    two_bands = shard_count == 4 and rest > 0
    inner = tiles - 2
    cuts = [(inner, [(2, OUTER, HALO)]), (1, [(1, OUTER, HALO)]), (1, [(tiles, OUTER, HALO)])]
    cuts += [(1, [((j,), None, half_rows), ((j,), OUTER, HALO)]) for j in col_sides]
    if two_bands:
        early = inner
        right = tiles - early - 1
        cuts += [(early, [(2, 5, rest)]), (1, [(1, 5, rest)]), (right, [(2 + early, 5, rest)])]
        cuts += [(inner, [(2, 6, HALO)]), (1, [(1, 6, HALO)]), (1, [(tiles, 6, HALO)])]
        cuts += [(tiles, [(1, 4, band)])]
    else:
        cuts += [(tiles, [(1, None, half_rows)]), (1, [(1, None, HALO)]), (1, [(1, None, HALO)])]
    full = (4, tiles + 2, height + 2 * HALO, LANE)
    ext, waves, lamp, near_tables, near_own, near_order = call(
        functools.partial(staging_kernel, sides),
        [
            block(*full),
            block(2, 2, PATCH, HALF),
            block(*probe_field.shape),
            jax.ShapeDtypeStruct(tables.shape, tables.dtype),
            block(*own.shape),
            jax.ShapeDtypeStruct(order.shape, order.dtype),
        ],
        [SMEM, ANY] + [VMEM] * (sides + 3) + [ANY] * 4,
        [VMEM] * 6,
        [pltpu.SemaphoreType.DMA((tiles + 4,))],
        own_info,
        planes,
        *col_halos,
        cosine,
        sine,
        order,
        probe_field,
        tables,
        own,
        order,
        limit=VMEM_LITTLE,
    )
    row_ends = call(
        functools.partial(corners_kernel, both),
        [block(both[0], 2, HALO, LANE)] * sides,
        [VMEM] * (1 + both[0]),
        [VMEM] * sides,
        [],
        near_order,
        *row_halos,
        limit=VMEM_LITTLE,
    )
    corner_halos = [to_cols(ends, j) for j, ends in zip(col_sides, row_ends)]
    arrivals = [peer, *row_halos, *corner_halos]
    copy_count = max(
        tiles * both[0], sum(len(parts) for _, parts in cuts)
    )
    outs = call(
        functools.partial(patches_kernel, both, [parts for _, parts in cuts]),
        [block(*full)] + [block(4, wide, sum(part[2] for part in parts), LANE) for wide, parts in cuts],
        [VMEM] + [ANY] * both[0] + [VMEM] * sides + [SMEM, SMEM] + [VMEM] * 6,
        [VMEM] + [ANY] * len(cuts),
        [
            pltpu.VMEM(full, jnp.float32),
            pltpu.SMEM((3 * (2 * PMAX + 1),), jnp.int32),
            *[
                pltpu.VMEM(shape, dtype)
                for _ in range(2)
                for shape, dtype in (
                    ((2, PATCH, GROUP // 2 * PATCH), jnp.bfloat16),
                    ((2, PATCH, GROUP // 2 * PATCH), jnp.float32),
                    ((2, GROUP // 2 * PATCH, PATCH), jnp.bfloat16),
                    ((2, GROUP // 2 * PATCH, PATCH), jnp.float32),
                    ((GROUP // 2, 2, PATCH, PATCH), jnp.float32),
                    ((GROUP // 2, 2, PATCH, PATCH), jnp.float32),
                )
            ],
            pltpu.VMEM((GROUP * PATCH, PATCH), jnp.float32),
            pltpu.SemaphoreType.DMA((copy_count,)),
        ],
        *arrivals,
        own_info,
        peer_info,
        ext,
        near_own,
        lamp,
        waves,
        near_tables,
        near_order,
        aliases={len(arrivals) + 2: 0},
    )[1:]
    outer_inner, outer_left, outer_right = outs[:3]
    rims, pieces = outs[3 : 3 + sides], outs[3 + sides :]

    def to_next(value):
        return joint_permute(
            value, ("row", "scan"), lambda r, s: (r + 1 if s < stride else r - 1, s)
        )

    def beside(value, mask=1):
        return lax.ppermute(value, "scan", [(i, i ^ mask) for i in range(shard_count)])

    def fold(kernel, out_shapes, *operands, scratch=()):
        many = isinstance(out_shapes, tuple)
        return call(
            functools.partial(kernel, height),
            out_shapes,
            [VMEM] * len(operands),
            (VMEM,) * len(out_shapes) if many else VMEM,
            list(scratch),
            *operands,
            limit=VMEM_LITTLE,
        )

    got_rims = [to_cols(rim, j) for j, rim in zip(col_sides, rims)]
    got_inner = to_next(outer_inner)
    open_edge, outer_edge = fold(
        lambda *refs: edge_kernel(refs[0], sides, *refs[1:]),
        (
            block(4, 1 + pieces[2].shape[1], pieces[1].shape[2], LANE),
            block(4, 2, HALO, LANE),
        ),
        pieces[1],
        pieces[2],
        outer_left,
        outer_right,
        *got_rims,
    )
    got_edge = to_next(outer_edge)
    if not two_bands:
        half = fold(
            lambda *refs: half_kernel(refs[0], sides, *refs[1:]),
            block(4, tiles, half_rows, LANE),
            pieces[0],
            got_inner,
            got_edge,
            *got_rims,
        )
        mask = stride // 2
        while mask > 0:
            size = half.shape[2] // 2
            low = (scan_at & mask) == 0
            keep = lax.dynamic_slice_in_dim(half, jnp.where(low, 0, size), size, axis=2)
            send = lax.dynamic_slice_in_dim(half, jnp.where(low, size, 0), size, axis=2)
            half = keep + beside(send, mask)
            mask //= 2
        return half.transpose(0, 2, 1, 3).reshape(2, 2, band, width)
    got_open = [beside(pieces[0]), beside(open_edge)]
    got_open[0], got_inner = lax.optimization_barrier((got_open[0], got_inner))
    got_open[1], got_edge = lax.optimization_barrier((got_open[1], got_edge))
    shut_inner = fold(shut_inner_kernel, block(4, inner, HALO, LANE), pieces[3], got_inner)
    got_shut = [beside(shut_inner)]
    shut_edge = fold(
        lambda *refs: shut_edge_kernel(refs[0], sides, *refs[1:]),
        block(4, 2, HALO, LANE),
        pieces[4],
        pieces[5],
        got_edge,
        *got_rims,
    )
    got_shut.append(beside(shut_edge))
    bulk, shut_rest = fold(
        lambda *refs: gather_kernel(refs[0], sides, *refs[1:]),
        (block(4, band, width), block(4, 2, HALO, LANE)),
        pieces[6],
        got_shut[0],
        *got_open,
        got_inner,
        got_edge,
        *got_rims,
        scratch=[pltpu.VMEM((4, tiles, band, LANE), jnp.float32)],
    )
    total = call(
        functools.partial(last_kernel, height),
        block(4, band, width),
        [ANY, VMEM, VMEM],
        ANY,
        [pltpu.VMEM((4, 2, HALO, LANE), jnp.float32), pltpu.SemaphoreType.DMA((2,))],
        bulk,
        shut_rest,
        got_shut[1],
        limit=VMEM_LITTLE,
        aliases={0: 0},
    )
    return total.reshape(2, 2, band, width)


def solution(mesh):
    placed = (
        P(None, None, "row", "col"),
        P(),
        P(),
        P("row", "col", "scan", None, None, None),
        P("row", "col", "scan", None, None),
        P("row", "col", "scan"),
    )
    return jax.shard_map(
        shards,
        mesh=mesh,
        in_specs=placed,
        out_specs=P(None, None, ("row", "scan"), "col"),
        check_vma=False,
    )
```

```python
import functools
import math

import jax
import jax.numpy as jnp
import numpy as np
from jax import lax
from jax.experimental import pallas as pl
from jax.experimental.pallas import tpu as pltpu
from jax.sharding import PartitionSpec as P

PATCH = 256
HALO = 64
PMAX = 3
LANE = 128
HALF = PATCH // 2
VMEM_LIMIT = 32 * 1024 * 1024
VMEM_LITTLE = 8 * 1024 * 1024
GROUP = 4
ROWS = 16


def block_tables():
    index = np.arange(HALF)
    tables = []
    for odd in range(2):
        angles = ((2 * index[:, None] + odd) * index[None, :] % PATCH) * (2.0 * math.pi / PATCH)
        cosines = np.cos(angles) / math.sqrt(PATCH)
        sines = np.sin(angles) / math.sqrt(PATCH)
        tables.append(np.block([[cosines, sines], [-sines, cosines]]))
    tables += [table.T for table in tables]
    return jnp.asarray(np.stack(tables).astype(np.float32)).astype(jnp.bfloat16)


def sorted_columns():
    index = np.arange(PATCH)
    matrix = np.zeros((PATCH, PATCH), np.float32)
    matrix[index, index % 2 * HALF + index // 2] = 1.0
    return jnp.asarray(np.stack([matrix, matrix.T])).astype(jnp.bfloat16)


def pair_of(index, phase):
    return index + 1 if index % 2 == phase else index - 1


def pairings(size):
    return range(1 if size <= 2 else 2)


def joint_permute(value, names, targets):
    sizes = [lax.axis_size(name) for name in names]
    route = []
    for flat in range(math.prod(sizes)):
        place = np.unravel_index(flat, sizes)
        goal = targets(*[int(i) for i in place])
        if goal is None or any(not 0 <= g < s for g, s in zip(goal, sizes)):
            continue
        route.append((flat, int(np.ravel_multi_index(goal, sizes))))
    return lax.ppermute(value, tuple(names) if len(names) > 1 else names[0], route)


OUTER = -1


def times(a, b):
    return jnp.dot(a, b, preferred_element_type=jnp.float32)


def side(parts, axis):
    return jnp.concatenate(parts, axis=axis)


def product(a, b):
    return a[0] * b[0] - a[1] * b[1], a[0] * b[1] + a[1] * b[0]


def conj_product(a, b):
    return a[0] * b[0] + a[1] * b[1], a[0] * b[1] - a[1] * b[0]


def by_lanes(multiply, a, b):
    pairs = [multiply([x[k] for x in a], [x[k] for x in b]) for k in range(2)]
    return [[pair[part] for pair in pairs] for part in range(2)]


def at_rows(start, count=ROWS):
    return slice(start, start + count)


def at_lanes(tile):
    return slice(tile * LANE, (tile + 1) * LANE)


def corner_of(row, col):
    return row + HALO, (col + LANE) // LANE, lax.rem(col + LANE, LANE)


class Patches:
    def __init__(self, x, y, p, z, near, far, tables):
        self.x, self.y, self.p, self.z, self.tables = x, y, p, z, tables
        self.near, self.far, self.count = near, far, near.shape[0]
        self.lane = lax.broadcasted_iota(jnp.int32, (ROWS, LANE), 1)

    def window(self, ext, slice_at, corner, start):
        top, tile, shift = corner_of(*corner)
        turn, inside = lax.rem(LANE - shift, LANE), self.lane < LANE - shift
        rows = pl.ds(top + start, ROWS)
        parts = []
        for plane in (2 * slice_at, 2 * slice_at + 1):
            moved = [pltpu.roll(ext[plane, tile + j, rows, :], turn, 1) for j in range(3)]
            parts.append([jnp.where(inside, moved[j], moved[j + 1]) for j in range(2)])
        return parts

    def deposit(self, acc, slice_at, corner, start, block, live):
        top, tile, shift = corner_of(*corner)
        inside, rows = self.lane >= shift, pl.ds(top + start, ROWS)
        for part in range(2):
            moved = [pltpu.roll(jnp.where(live, b, 0.0), shift, 1) for b in block[part]]
            sums = [
                jnp.where(inside, moved[0], 0.0),
                jnp.where(inside, moved[1], moved[0]),
                jnp.where(inside, 0.0, moved[1]),
            ]
            for j in range(3):
                acc[2 * slice_at + part, tile + j, rows, :] += sums[j]

    def fill(self, i, row, blocks):
        for part in range(2):
            for k in range(2):
                low, high = blocks[0][part][k], blocks[1][part][k]
                rows, lanes = at_rows(part * HALF + row), at_lanes(2 * i + k)
                self.x[0, rows, lanes] = (low + high).astype(jnp.bfloat16)
                self.x[1, rows, lanes] = (low - high).astype(jnp.bfloat16)

    def multiply_left(self, *tables):
        for odd, table in enumerate(tables):
            for i in range(self.count):
                part = slice(i * PATCH, (i + 1) * PATCH)
                self.y[odd, :, part] = times(table, self.x[odd, :, part])
            yield

    def multiply_right(self, *tables):
        for odd, table in enumerate(tables):
            self.z[odd] = times(self.p[odd], table)
            yield

    def to_frequencies(self):
        yield from self.multiply_left(self.tables[0], self.tables[1])
        for i in range(self.count):
            for a in range(2):
                for row in range(0, HALF, ROWS):
                    for part in range(2):
                        rows = at_rows(part * HALF + row)
                        low, high = [self.y[a, rows, at_lanes(2 * i + k)] for k in range(2)]
                        rows = at_rows((2 * i + a) * HALF + row)
                        self.p[0, rows, at_lanes(part)] = (low + high).astype(jnp.bfloat16)
                        self.p[1, rows, at_lanes(part)] = (low - high).astype(jnp.bfloat16)
            yield
        yield from self.multiply_right(self.tables[2], self.tables[3])

    def change(self, function):
        for i in range(self.count):
            for a in range(2):
                for row in range(0, HALF, ROWS):
                    rows = at_rows((2 * i + a) * HALF + row)
                    for b in range(2):
                        value = [self.z[b, rows, at_lanes(part)] for part in range(2)]
                        result = function(i, b, a * HALF + row, value)
                        for part in range(2):
                            to = at_rows(part * HALF + row)
                            self.x[a, to, at_lanes(2 * i + b)] = result[part].astype(jnp.bfloat16)
            yield

    def from_frequencies(self):
        yield from self.multiply_left(self.tables[2], self.tables[3])
        for i in range(self.count):
            for b in range(2):
                for row in range(0, HALF, ROWS):
                    for part in range(2):
                        rows = at_rows(part * HALF + row)
                        even, odd = [self.y[a, rows, at_lanes(2 * i + b)] for a in range(2)]
                        rows = [at_rows((2 * i + half) * HALF + row) for half in range(2)]
                        self.p[b, rows[0], at_lanes(part)] = (even + odd).astype(jnp.bfloat16)
                        self.p[b, rows[1], at_lanes(part)] = (even - odd).astype(jnp.bfloat16)
            yield
        yield from self.multiply_right(self.tables[0], self.tables[1])

    def result(self, i, half, row):
        rows, parts = at_rows((2 * i + half) * HALF + row), []
        for part in range(2):
            even, odd = [self.z[b, rows, at_lanes(part)] for b in range(2)]
            parts.append([even + odd, even - odd])
        return parts

    def last(self, row):
        return row + ROWS == HALF

    def blocks(self):
        return [(i, row) for i in range(self.count) for row in range(0, HALF, ROWS)]


def block_of(ref, i, half, row):
    rows = at_rows(half * HALF + row)
    return [[ref[i, part, rows, at_lanes(k)] for k in range(2)] for part in range(2)]


def keep_block(ref, i, half, row, block):
    rows = at_rows(half * HALF + row)
    for part in range(2):
        for k in range(2):
            ref[i, part, rows, at_lanes(k)] = block[part][k]


def patch_gradients(patches, ext, acc, corners, lives, intensity, probe, waves):
    near, far = patches.near, patches.far

    def lamp(half, row):
        rows = at_rows(half * HALF + row)
        return [[probe[part, rows, at_lanes(k)] for k in range(2)] for part in range(2)]

    def prop(b, row):
        return [waves[part, b, at_rows(row), :] for part in range(2)]

    for i, row in patches.blocks():
        patches.fill(
            i,
            row,
            [
                by_lanes(
                    product, lamp(half, row), patches.window(ext, 0, corners[i], half * HALF + row)
                )
                for half in range(2)
            ],
        )
        if patches.last(row):
            yield
    yield from patches.to_frequencies()
    yield from patches.change(lambda i, b, row, z: product(prop(b, row), z))
    yield from patches.from_frequencies()
    for i, row in patches.blocks():
        leaving = []
        for half in range(2):
            arrived = patches.result(i, half, row)
            second = patches.window(ext, 1, corners[i], half * HALF + row)
            keep_block(near, i, half, row, arrived)
            keep_block(far, i, half, row, second)
            leaving.append(by_lanes(product, second, arrived))
        patches.fill(i, row, leaving)
        if patches.last(row):
            yield
    yield from patches.to_frequencies()

    def residual(i, b, row, z):
        misfit = z[0] * z[0] + z[1] * z[1] - intensity[at_rows(i * PATCH + row), at_lanes(b)]
        return misfit * z[0], misfit * z[1]

    yield from patches.change(residual)
    yield from patches.from_frequencies()
    for i, row in patches.blocks():
        through = []
        for half in range(2):
            back = patches.result(i, half, row)
            start = half * HALF + row
            grad = by_lanes(conj_product, block_of(near, i, half, row), back)
            patches.deposit(acc, 1, corners[i], start, grad, lives[i])
            through.append(by_lanes(conj_product, block_of(far, i, half, row), back))
        patches.fill(i, row, through)
        if patches.last(row):
            yield
    yield from patches.to_frequencies()
    yield from patches.change(lambda i, b, row, z: conj_product(prop(b, row), z))
    yield from patches.from_frequencies()
    for i, row in patches.blocks():
        for half in range(2):
            grad = by_lanes(conj_product, lamp(half, row), patches.result(i, half, row))
            patches.deposit(acc, 0, corners[i], half * HALF + row, grad, lives[i])
        if patches.last(row):
            yield


def in_turns(first, second):
    for _ in range(GROUP // 2):
        next(first)
    going = [first, second]
    while going:
        for group in list(going):
            try:
                next(group)
            except StopIteration:
                going.remove(group)


def place_of(height):
    shard_count = lax.axis_size("scan")
    scan_at = lax.axis_index("scan")
    band = height // shard_count
    upper = scan_at < shard_count // 2
    even = scan_at % 2 == 0
    open_at = jnp.where(upper, HALO, 0)
    shut_at = jnp.where(upper, 0, band - HALO)
    other_at = jnp.where(even, band, 0)
    return [
        jnp.where(upper, 0, height // 2),
        jnp.where(upper, height, -HALO),
        lax.axis_index("row") % 2,
        lax.axis_index("col") % 2,
        jnp.where(even, 0, band),
        other_at + open_at,
        other_at + shut_at,
        ((scan_at == 0) | (scan_at == shard_count - 1)).astype(jnp.int32),
        shut_at,
        open_at,
    ]


def wanted(place, row, half_rows):
    inner = (row < place[0] + half_rows) & (row + PATCH > place[0])
    outer = (row < place[1] + HALO) & (row + PATCH > place[1])
    return inner | outer


def far_tile(place, phase, tiles):
    return jnp.where(place[3] == phase, tiles - 1, 0)


class Copies:
    def __init__(self, sems):
        self.sems, self.all = sems, []

    def start(self, source, target):
        copy = pltpu.make_async_copy(source, target, self.sems.at[len(self.all)])
        copy.start()
        self.all.append(copy)
        return copy

    def wait(self):
        for copy in self.all:
            copy.wait()


def staging_kernel(sides, _, core, *refs):
    col_refs, refs = refs[:sides], refs[sides:]
    cosine, sine, order, near, (ext, waves, *near_to), sems = *refs[:3], refs[3:7], refs[7:-1], refs[-1]
    for k, wave in enumerate((cosine, sine)):
        sorted_wave = sort_frequencies([wave[...]], order)
        for odd in range(2):
            waves[k, odd] = sorted_wave[:, odd * HALF : (odd + 1) * HALF]
    height, width = core.shape[1], core.shape[2]
    tiles = ext.shape[1]
    place = place_of(height)
    copies = Copies(sems)
    for t in range(width // LANE):
        part = core.at[:, :, pl.ds(t * LANE, LANE)]
        copies.start(part, ext.at[:, t + 1, pl.ds(HALO, height), :])
    for source, target in zip(near, near_to):
        copies.start(source, target)
    for j, ref in enumerate(col_refs):
        tile = far_tile(place, j, tiles)
        for p in range(2):
            for k, half in enumerate(unpacked(ref[p], place[3] != j)):
                ext[p + 2 * k, tile, HALO : HALO + height, :] = half
    copies.wait()


def ready_kernel(sides, *refs):
    row_refs, refs = refs[: sides[0]], refs[sides[0] :]
    corner_refs, (ext, _, acc) = refs[: sides[1]], refs[sides[1] :]
    tiles, height = ext.shape[1], ext.shape[2] - 2 * HALO
    place = place_of(height)

    def far_row(phase):
        return pl.ds(pl.multiple_of(jnp.where(place[2] == phase, height + HALO, 0), 8), HALO)

    for i, ref in enumerate(row_refs):
        for t in range(tiles - 2):
            ext[:, t + 1, far_row(i), :] = ref[:, :, at_lanes(t)]
    for j, ref in enumerate(corner_refs):
        tile = far_tile(place, j, tiles)
        for i in range(sides[0]):
            for p in range(2):
                for q, half in enumerate(unpacked(ref[i, p], place[3] != j)):
                    ext[p + 2 * q, tile, far_row(i), :] = half
    for start, count in ((place[0], height // 2), (place[1], HALO)):
        rows = pl.ds(pl.multiple_of(start + HALO, 8), count)
        acc[:, :, rows, :] = jnp.zeros((4, tiles, count, LANE), jnp.float32)


def patches_kernel(cuts, peer, *refs):
    own_info, peer_info, ext, acc, own, probe, waves, tables, order = refs[:9]
    outs, (queue, *scratch, ordered, sems) = refs[10:-15], refs[-15:]
    groups = [Patches(*scratch[:6], tables), Patches(*scratch[6:], tables)]
    tiles, height = ext.shape[1], ext.shape[2] - 2 * HALO
    half_rows = height // 2
    place = place_of(height)
    first = pl.multiple_of(place[0] + HALO, 8)
    outer = pl.multiple_of(place[1] + HALO, 8)

    def intensity(index):
        mine, theirs = jnp.minimum(index, PMAX - 1), jnp.maximum(index - PMAX, 0)
        return jnp.where(index < PMAX, own[mine], peer[theirs])

    length = jnp.int32(0)
    for index in range(2 * PMAX):
        info, slot = (own_info, index) if index < PMAX else (peer_info, index - PMAX)
        row, col, count = info[slot], info[PMAX + slot], info[2 * PMAX]
        queue[3 * length] = index
        queue[3 * length + 1] = row
        queue[3 * length + 2] = col
        length = length + ((slot < count) & wanted(place, row, half_rows)).astype(jnp.int32)

    def step(turn_at, carry):
        start = GROUP * turn_at
        items = [start] + [jnp.minimum(start + i, length - 1) for i in range(1, GROUP)]
        corners = [(queue[3 * i + 1], queue[3 * i + 2]) for i in items]
        lives = [start + i < length for i in range(GROUP)]
        ordered[...] = sort_frequencies([intensity(queue[3 * i]) for i in items], order)
        steps = []
        for k, patches in enumerate(groups):
            part = slice(k * patches.count, (k + 1) * patches.count)
            intensities = ordered.at[pl.ds(k * patches.count * PATCH, patches.count * PATCH)]
            steps.append(
                patch_gradients(
                    patches, ext, acc, corners[part], lives[part], intensities, probe, waves
                )
            )
        in_turns(*steps)
        return carry

    lax.fori_loop(0, (length + GROUP - 1) // GROUP, step, 0)
    gifts = Copies(sems)
    for target, parts in zip(outs, cuts):
        row_to = 0
        for tile, at, count in parts:
            tile = far_tile(place, tile[0], tiles) if isinstance(tile, tuple) else tile
            row = outer if at == OUTER else first
            row = row if at in (OUTER, None) else pl.multiple_of(first + place[at], 8)
            gifts.start(
                acc.at[:, pl.ds(tile, target.shape[1]), pl.ds(row, count), :],
                target.at[:, :, pl.ds(row_to, count), :],
            )
            row_to += count
    gifts.wait()


def near_tile(place, phase, tiles):
    return jnp.where(place[3] == phase, tiles - 1, 0)


def add_rims(place, out, rims, rim_row):
    _, tiles, rows, _ = out.shape
    for j, rim in enumerate(rims):
        at = near_tile(place, j, tiles)
        out[:, at, :, :] += rim[:, 0, pl.ds(rim_row, rows), :]


def edge_kernel(height, sides, open_left, open_right, outer_left, outer_right, *refs):
    place = place_of(height)
    rims, (open_out, outer_out) = refs[:sides], refs[-2:]
    open_out[:, 0:1] = open_left[...]
    open_out[:, 1:] = open_right[...]
    add_rims(place, open_out, rims, pl.multiple_of(place[5], 8))
    outer_out[:, 0:1] = outer_left[...]
    outer_out[:, 1:2] = outer_right[...]
    add_rims(place, outer_out, rims, height // 2)


def shut_inner_kernel(height, part, strip, out):
    place = place_of(height)
    out[...] = part[...]

    @pl.when(place[7] == 0)
    def _():
        out[...] += strip[...]


def shut_edge_kernel(height, sides, left, right, strip, *refs):
    place = place_of(height)
    rims, out = refs[:sides], refs[sides]
    out[:, 0:1] = left[...]
    out[:, 1:2] = right[...]
    add_rims(place, out, rims, pl.multiple_of(place[6], 8))

    @pl.when(place[7] == 0)
    def _():
        out[...] += strip[...]


def gather_kernel(height, sides, part, *refs):
    place = place_of(height)
    shut_got, open_got, strip, rims = refs[0], refs[1:3], refs[3:5], refs[5 : 5 + sides]
    out, edge_out, work = refs[5 + sides :]
    work[...] = part[...]
    tiles = work.shape[1]
    add_rims(place, work, rims, pl.multiple_of(place[4], 8))

    def add(at, inner, edge=None):
        rows = pl.ds(pl.multiple_of(at, 8), inner.shape[2])
        split = 1 + inner.shape[1]
        work[:, 1:split, rows, :] += inner[...]
        if edge is not None:
            work[:, 0:1, rows, :] += edge[:, 0:1]
            work[:, split:, rows, :] += edge[:, 1:]

    add(place[9], *open_got)
    add(place[8], shut_got)

    @pl.when(place[7] == 1)
    def _():
        add(place[8], *strip)

    shut_rows = pl.ds(pl.multiple_of(place[8], 8), HALO)
    edge_out[:, 0:1] = work[:, 0:1, shut_rows, :]
    edge_out[:, 1:2] = work[:, tiles - 1 :, shut_rows, :]
    for t in range(tiles):
        out[:, :, t * LANE : (t + 1) * LANE] = work[:, t]


def last_kernel(height, total, edge, got, out, work, sems):
    place = place_of(height)
    rows = pl.ds(pl.multiple_of(place[8], 8), HALO)
    work[...] = edge[...] + got[...]
    copies = Copies(sems)
    for k in range(2):
        lanes = pl.ds(k * (out.shape[2] - LANE), LANE)
        copies.start(work.at[:, k], out.at[:, rows, lanes])
    copies.wait()


def half_kernel(height, sides, part, inner, edge, *refs):
    place = place_of(height)
    rims, out = refs[:sides], refs[sides]
    out[...] = part[...]
    add_rims(place, out, rims, 0)
    tiles = out.shape[1]
    rows = pl.ds(pl.multiple_of(jnp.where(place[0] == 0, 0, out.shape[2] - HALO), 8), HALO)
    out[:, 1 : tiles - 1, rows, :] += inner[...]
    out[:, 0:1, rows, :] += edge[:, 0:1]
    out[:, tiles - 1 : tiles, rows, :] += edge[:, 1:2]


def near_rows(place, phase, height):
    return pl.ds(pl.multiple_of(jnp.where(place[2] == phase, height - HALO, 0), HALO), HALO)


def near_cols(place, phase, width):
    return pl.ds(pl.multiple_of(jnp.where(place[3] == phase, width - LANE, 0), LANE), LANE)


def sort_frequencies(arrays, order):
    values = side(arrays, 1)
    total = None
    for _ in range(3):
        part = values.astype(jnp.bfloat16)
        values = values - part.astype(jnp.float32)
        rows = times(order[1], part).astype(jnp.bfloat16)
        rows = side([rows[:, i * PATCH : (i + 1) * PATCH] for i in range(len(arrays))], 0)
        moved = times(rows, order[0])
        total = moved if total is None else total + moved
    return total


def packed(strips, high):
    low_lanes = lax.broadcasted_iota(jnp.int32, strips[0].shape, 1) < HALO
    turns = [jnp.where(high, LANE - HALO, 0), jnp.where(high, 0, HALO)]
    parts = [pltpu.roll(strip, turn, 1) for strip, turn in zip(strips, turns)]
    return jnp.where(low_lanes, *parts)


def unpacked(tile, high):
    return [
        pltpu.roll(tile, turn, 1)
        for turn in (jnp.where(high, HALO, 0), jnp.where(high, 0, LANE - HALO))
    ]


def edges_kernel(sides, core, *refs):
    outs, (cols, sems) = refs[:-2], refs[-2:]
    copies = Copies(sems)
    height, width = core.shape[1:]
    place = place_of(height)
    for j in range(sides[1]):
        copies.start(core.at[:, :, near_cols(place, j, width)], cols.at[j])
    for i in range(sides[0]):
        copies.start(core.at[:, near_rows(place, i, height), :], outs[i])
    copies.wait()
    for j in range(sides[1]):
        high = place[3] == j
        for p in range(2):
            outs[sides[0] + j][p] = packed([cols[j, p], cols[j, p + 2]], high)


def corners_kernel(sides, _, *refs):
    strips, outs = refs[: sides[0]], refs[sides[0] :]
    width = strips[0].shape[2]
    for j, out in enumerate(outs):
        high = lax.axis_index("col") % 2 == j
        cols = pl.ds(pl.multiple_of(jnp.where(high, width - LANE, 0), LANE), LANE)
        for i, strip in enumerate(strips):
            for p in range(2):
                out[i, p] = packed([strip[p, :, cols], strip[p + 2, :, cols]], high)


ANY = pl.BlockSpec(memory_space=pl.ANY)
VMEM = pl.BlockSpec(memory_space=pltpu.VMEM)
SMEM = pl.BlockSpec(memory_space=pltpu.SMEM)


def block(*shape):
    return jax.ShapeDtypeStruct(shape, jnp.float32)


def call(kernel, out_shapes, in_specs, out_specs, scratch, *operands, limit=VMEM_LIMIT, aliases=None):
    return pl.pallas_call(
        kernel,
        out_shape=out_shapes,
        in_specs=in_specs,
        out_specs=out_specs,
        scratch_shapes=scratch,
        input_output_aliases=aliases or {},
        compiler_params=pltpu.CompilerParams(vmem_limit_bytes=limit),
        cost_estimate=pl.CostEstimate(flops=0, bytes_accessed=0, transcendentals=0),
    )(*operands)


def shards(object_field, probe_field, prop_phase, measured, positions, counts):
    height, width = object_field.shape[2:]
    shard_count = lax.axis_size("scan")
    half_rows = height // 2
    band = height // shard_count
    rest = band - HALO
    tiles = width // LANE
    row_sides = pairings(lax.axis_size("row"))
    col_sides = pairings(lax.axis_size("col"))
    sides = len(col_sides)
    both = (len(row_sides), sides)
    stride = shard_count // 2
    scan_at = lax.axis_index("scan")
    planes = object_field.reshape(4, height, width)
    own = measured.reshape(PMAX, PATCH, PATCH)
    order = sorted_columns()
    own_info = jnp.concatenate(
        [positions.reshape(PMAX, 2).T.reshape(-1), counts.reshape(1), jnp.zeros((1,), jnp.int32)]
    ).astype(jnp.int32)

    def across(value):
        return lax.ppermute(value, "scan", [(i, i ^ stride) for i in range(shard_count)])

    def to_cols(value, j):
        return joint_permute(value, ("col",), lambda c: (pair_of(c, j),))

    def to_rows(value, i):
        return joint_permute(value, ("row",), lambda r: (pair_of(r, i),))

    peer = across(own)
    peer_info = across(own_info)
    edge_shapes = (
        [block(4, HALO, width)] * both[0]
        + [block(2, height, LANE)] * sides
    )
    edges = call(
        functools.partial(edges_kernel, both),
        edge_shapes,
        [ANY],
        [VMEM] * len(edge_shapes),
        [pltpu.VMEM((sides, 4, height, LANE), jnp.float32), pltpu.SemaphoreType.DMA((sum(both),))],
        planes,
        limit=VMEM_LITTLE,
    )
    row_halos = [to_rows(edges[i], i) for i in row_sides]
    col_halos = [to_cols(edges[both[0] + j], j) for j in col_sides]
    cosine, sine = jnp.cos(prop_phase), jnp.sin(prop_phase)
    tables = block_tables()

    two_bands = shard_count == 4 and rest > 0
    inner = tiles - 2
    cuts = [(inner, [(2, OUTER, HALO)]), (1, [(1, OUTER, HALO)]), (1, [(tiles, OUTER, HALO)])]
    cuts += [(1, [((j,), None, half_rows), ((j,), OUTER, HALO)]) for j in col_sides]
    if two_bands:
        early = inner
        right = tiles - early - 1
        cuts += [(early, [(2, 5, rest)]), (1, [(1, 5, rest)]), (right, [(2 + early, 5, rest)])]
        cuts += [(inner, [(2, 6, HALO)]), (1, [(1, 6, HALO)]), (1, [(tiles, 6, HALO)])]
        cuts += [(tiles, [(1, 4, band)])]
    else:
        cuts += [(tiles, [(1, None, half_rows)]), (1, [(1, None, HALO)]), (1, [(1, None, HALO)])]
    full = (4, tiles + 2, height + 2 * HALO, LANE)
    ext, waves, lamp, near_tables, near_own, near_order = call(
        functools.partial(staging_kernel, sides),
        [
            block(*full),
            block(2, 2, PATCH, HALF),
            block(*probe_field.shape),
            jax.ShapeDtypeStruct(tables.shape, tables.dtype),
            block(*own.shape),
            jax.ShapeDtypeStruct(order.shape, order.dtype),
        ],
        [SMEM, ANY] + [VMEM] * (sides + 3) + [ANY] * 4,
        [VMEM] * 6,
        [pltpu.SemaphoreType.DMA((tiles + 4,))],
        own_info,
        planes,
        *col_halos,
        cosine,
        sine,
        order,
        probe_field,
        tables,
        own,
        order,
        limit=VMEM_LITTLE,
    )
    row_ends = call(
        functools.partial(corners_kernel, both),
        [block(both[0], 2, HALO, LANE)] * sides,
        [VMEM] * (1 + both[0]),
        [VMEM] * sides,
        [],
        near_order,
        *row_halos,
        limit=VMEM_LITTLE,
    )
    corner_halos = [to_cols(ends, j) for j, ends in zip(col_sides, row_ends)]
    ext, acc = call(
        functools.partial(ready_kernel, both),
        [block(*full), block(*full)],
        [VMEM] * (both[0] + sides + 1),
        [VMEM, VMEM],
        [],
        *row_halos,
        *corner_halos,
        ext,
        limit=VMEM_LITTLE,
        aliases={both[0] + sides: 0},
    )
    outs = call(
        functools.partial(patches_kernel, [parts for _, parts in cuts]),
        [block(*full)] + [block(4, wide, sum(part[2] for part in parts), LANE) for wide, parts in cuts],
        [VMEM, SMEM, SMEM] + [VMEM] * 7,
        [VMEM] + [ANY] * len(cuts),
        [
            pltpu.SMEM((3 * (2 * PMAX + 1),), jnp.int32),
            *[
                pltpu.VMEM(shape, dtype)
                for _ in range(2)
                for shape, dtype in (
                    ((2, PATCH, GROUP // 2 * PATCH), jnp.bfloat16),
                    ((2, PATCH, GROUP // 2 * PATCH), jnp.float32),
                    ((2, GROUP // 2 * PATCH, PATCH), jnp.bfloat16),
                    ((2, GROUP // 2 * PATCH, PATCH), jnp.float32),
                    ((GROUP // 2, 2, PATCH, PATCH), jnp.float32),
                    ((GROUP // 2, 2, PATCH, PATCH), jnp.float32),
                )
            ],
            pltpu.VMEM((GROUP * PATCH, PATCH), jnp.float32),
            pltpu.SemaphoreType.DMA((sum(len(parts) for _, parts in cuts),)),
        ],
        peer,
        own_info,
        peer_info,
        ext,
        acc,
        near_own,
        lamp,
        waves,
        near_tables,
        near_order,
        aliases={4: 0},
    )[1:]
    outer_inner, outer_left, outer_right = outs[:3]
    rims, pieces = outs[3 : 3 + sides], outs[3 + sides :]

    def to_next(value):
        return joint_permute(
            value, ("row", "scan"), lambda r, s: (r + 1 if s < stride else r - 1, s)
        )

    def beside(value, mask=1):
        return lax.ppermute(value, "scan", [(i, i ^ mask) for i in range(shard_count)])

    def fold(kernel, out_shapes, *operands, scratch=()):
        many = isinstance(out_shapes, tuple)
        return call(
            functools.partial(kernel, height),
            out_shapes,
            [VMEM] * len(operands),
            (VMEM,) * len(out_shapes) if many else VMEM,
            list(scratch),
            *operands,
            limit=VMEM_LITTLE,
        )

    got_rims = [to_cols(rim, j) for j, rim in zip(col_sides, rims)]
    got_inner = to_next(outer_inner)
    open_edge, outer_edge = fold(
        lambda *refs: edge_kernel(refs[0], sides, *refs[1:]),
        (
            block(4, 1 + pieces[2].shape[1], pieces[1].shape[2], LANE),
            block(4, 2, HALO, LANE),
        ),
        pieces[1],
        pieces[2],
        outer_left,
        outer_right,
        *got_rims,
    )
    got_edge = to_next(outer_edge)
    if not two_bands:
        half = fold(
            lambda *refs: half_kernel(refs[0], sides, *refs[1:]),
            block(4, tiles, half_rows, LANE),
            pieces[0],
            got_inner,
            got_edge,
            *got_rims,
        )
        mask = stride // 2
        while mask > 0:
            size = half.shape[2] // 2
            low = (scan_at & mask) == 0
            keep = lax.dynamic_slice_in_dim(half, jnp.where(low, 0, size), size, axis=2)
            send = lax.dynamic_slice_in_dim(half, jnp.where(low, size, 0), size, axis=2)
            half = keep + beside(send, mask)
            mask //= 2
        return half.transpose(0, 2, 1, 3).reshape(2, 2, band, width)
    got_open = [beside(pieces[0]), beside(open_edge)]
    got_open[0], got_inner = lax.optimization_barrier((got_open[0], got_inner))
    got_open[1], got_edge = lax.optimization_barrier((got_open[1], got_edge))
    shut_inner = fold(shut_inner_kernel, block(4, inner, HALO, LANE), pieces[3], got_inner)
    got_shut = [beside(shut_inner)]
    shut_edge = fold(
        lambda *refs: shut_edge_kernel(refs[0], sides, *refs[1:]),
        block(4, 2, HALO, LANE),
        pieces[4],
        pieces[5],
        got_edge,
        *got_rims,
    )
    got_shut.append(beside(shut_edge))
    bulk, shut_rest = fold(
        lambda *refs: gather_kernel(refs[0], sides, *refs[1:]),
        (block(4, band, width), block(4, 2, HALO, LANE)),
        pieces[6],
        got_shut[0],
        *got_open,
        got_inner,
        got_edge,
        *got_rims,
        scratch=[pltpu.VMEM((4, tiles, band, LANE), jnp.float32)],
    )
    total = call(
        functools.partial(last_kernel, height),
        block(4, band, width),
        [ANY, VMEM, VMEM],
        ANY,
        [pltpu.VMEM((4, 2, HALO, LANE), jnp.float32), pltpu.SemaphoreType.DMA((2,))],
        bulk,
        shut_rest,
        got_shut[1],
        limit=VMEM_LITTLE,
        aliases={0: 0},
    )
    return total.reshape(2, 2, band, width)


def solution(mesh):
    placed = (
        P(None, None, "row", "col"),
        P(),
        P(),
        P("row", "col", "scan", None, None, None),
        P("row", "col", "scan", None, None),
        P("row", "col", "scan"),
    )
    return jax.shard_map(
        shards,
        mesh=mesh,
        in_specs=placed,
        out_specs=P(None, None, ("row", "scan"), "col"),
        check_vma=False,
    )
```

```python
import functools
import math

import jax
import jax.numpy as jnp
import numpy as np
from jax import lax
from jax.experimental import pallas as pl
from jax.experimental.pallas import tpu as pltpu
from jax.sharding import PartitionSpec as P

PATCH = 256
HALO = 64
PMAX = 3
LANE = 128
HALF = PATCH // 2
VMEM_LIMIT = 32 * 1024 * 1024
VMEM_LITTLE = 8 * 1024 * 1024
GROUP = 4
ROWS = 16


def block_tables():
    index = np.arange(HALF)
    tables = []
    for odd in range(2):
        angles = ((2 * index[:, None] + odd) * index[None, :] % PATCH) * (2.0 * math.pi / PATCH)
        cosines = np.cos(angles) / math.sqrt(PATCH)
        sines = np.sin(angles) / math.sqrt(PATCH)
        tables.append(np.block([[cosines, sines], [-sines, cosines]]))
    tables += [table.T for table in tables]
    return jnp.asarray(np.stack(tables).astype(np.float32)).astype(jnp.bfloat16)


def sorted_columns():
    index = np.arange(PATCH)
    matrix = np.zeros((PATCH, PATCH), np.float32)
    matrix[index, index % 2 * HALF + index // 2] = 1.0
    return jnp.asarray(np.stack([matrix, matrix.T])).astype(jnp.bfloat16)


def pair_of(index, phase):
    return index + 1 if index % 2 == phase else index - 1


def pairings(size):
    return range(1 if size <= 2 else 2)


def joint_permute(value, names, targets):
    sizes = [lax.axis_size(name) for name in names]
    route = []
    for flat in range(math.prod(sizes)):
        place = np.unravel_index(flat, sizes)
        goal = targets(*[int(i) for i in place])
        if goal is None or any(not 0 <= g < s for g, s in zip(goal, sizes)):
            continue
        route.append((flat, int(np.ravel_multi_index(goal, sizes))))
    return lax.ppermute(value, tuple(names) if len(names) > 1 else names[0], route)


OUTER = -1


def times(a, b):
    return jnp.dot(a, b, preferred_element_type=jnp.float32)


def side(parts, axis):
    return jnp.concatenate(parts, axis=axis)


def product(a, b):
    return a[0] * b[0] - a[1] * b[1], a[0] * b[1] + a[1] * b[0]


def conj_product(a, b):
    return a[0] * b[0] + a[1] * b[1], a[0] * b[1] - a[1] * b[0]


def by_lanes(multiply, a, b):
    pairs = [multiply([x[k] for x in a], [x[k] for x in b]) for k in range(2)]
    return [[pair[part] for pair in pairs] for part in range(2)]


def at_rows(start, count=ROWS):
    return slice(start, start + count)


def at_lanes(tile):
    return slice(tile * LANE, (tile + 1) * LANE)


def corner_of(row, col):
    return row + HALO, (col + LANE) // LANE, lax.rem(col + LANE, LANE)


class Patches:
    def __init__(self, x, y, p, z, near, far, tables):
        self.x, self.y, self.p, self.z, self.tables = x, y, p, z, tables
        self.near, self.far, self.count = near, far, near.shape[0]
        self.lane = lax.broadcasted_iota(jnp.int32, (ROWS, LANE), 1)

    def window(self, ext, slice_at, corner, start):
        top, tile, shift = corner_of(*corner)
        turn, inside = lax.rem(LANE - shift, LANE), self.lane < LANE - shift
        rows = pl.ds(top + start, ROWS)
        parts = []
        for plane in (2 * slice_at, 2 * slice_at + 1):
            moved = [pltpu.roll(ext[plane, tile + j, rows, :], turn, 1) for j in range(3)]
            parts.append([jnp.where(inside, moved[j], moved[j + 1]) for j in range(2)])
        return parts

    def deposit(self, acc, slice_at, corner, start, block, live):
        top, tile, shift = corner_of(*corner)
        inside, rows = self.lane >= shift, pl.ds(top + start, ROWS)
        for part in range(2):
            moved = [pltpu.roll(jnp.where(live, b, 0.0), shift, 1) for b in block[part]]
            sums = [
                jnp.where(inside, moved[0], 0.0),
                jnp.where(inside, moved[1], moved[0]),
                jnp.where(inside, 0.0, moved[1]),
            ]
            for j in range(3):
                acc[2 * slice_at + part, tile + j, rows, :] += sums[j]

    def fill(self, i, row, blocks):
        for part in range(2):
            for k in range(2):
                low, high = blocks[0][part][k], blocks[1][part][k]
                rows, lanes = at_rows(part * HALF + row), at_lanes(2 * i + k)
                self.x[0, rows, lanes] = (low + high).astype(jnp.bfloat16)
                self.x[1, rows, lanes] = (low - high).astype(jnp.bfloat16)

    def multiply_left(self, *tables):
        for odd, table in enumerate(tables):
            for i in range(self.count):
                part = slice(i * PATCH, (i + 1) * PATCH)
                self.y[odd, :, part] = times(table, self.x[odd, :, part])
            yield

    def multiply_right(self, *tables):
        for odd, table in enumerate(tables):
            self.z[odd] = times(self.p[odd], table)
            yield

    def to_frequencies(self):
        yield from self.multiply_left(self.tables[0], self.tables[1])
        for i in range(self.count):
            for a in range(2):
                for row in range(0, HALF, ROWS):
                    for part in range(2):
                        rows = at_rows(part * HALF + row)
                        low, high = [self.y[a, rows, at_lanes(2 * i + k)] for k in range(2)]
                        rows = at_rows((2 * i + a) * HALF + row)
                        self.p[0, rows, at_lanes(part)] = (low + high).astype(jnp.bfloat16)
                        self.p[1, rows, at_lanes(part)] = (low - high).astype(jnp.bfloat16)
            yield
        yield from self.multiply_right(self.tables[2], self.tables[3])

    def change(self, function):
        for i in range(self.count):
            for a in range(2):
                for row in range(0, HALF, ROWS):
                    rows = at_rows((2 * i + a) * HALF + row)
                    for b in range(2):
                        value = [self.z[b, rows, at_lanes(part)] for part in range(2)]
                        result = function(i, b, a * HALF + row, value)
                        for part in range(2):
                            to = at_rows(part * HALF + row)
                            self.x[a, to, at_lanes(2 * i + b)] = result[part].astype(jnp.bfloat16)
            yield

    def from_frequencies(self):
        yield from self.multiply_left(self.tables[2], self.tables[3])
        for i in range(self.count):
            for b in range(2):
                for row in range(0, HALF, ROWS):
                    for part in range(2):
                        rows = at_rows(part * HALF + row)
                        even, odd = [self.y[a, rows, at_lanes(2 * i + b)] for a in range(2)]
                        rows = [at_rows((2 * i + half) * HALF + row) for half in range(2)]
                        self.p[b, rows[0], at_lanes(part)] = (even + odd).astype(jnp.bfloat16)
                        self.p[b, rows[1], at_lanes(part)] = (even - odd).astype(jnp.bfloat16)
            yield
        yield from self.multiply_right(self.tables[0], self.tables[1])

    def result(self, i, half, row):
        rows, parts = at_rows((2 * i + half) * HALF + row), []
        for part in range(2):
            even, odd = [self.z[b, rows, at_lanes(part)] for b in range(2)]
            parts.append([even + odd, even - odd])
        return parts

    def last(self, row):
        return row + ROWS == HALF

    def blocks(self):
        return [(i, row) for i in range(self.count) for row in range(0, HALF, ROWS)]


def block_of(ref, i, half, row):
    rows = at_rows(half * HALF + row)
    return [[ref[i, part, rows, at_lanes(k)] for k in range(2)] for part in range(2)]


def keep_block(ref, i, half, row, block):
    rows = at_rows(half * HALF + row)
    for part in range(2):
        for k in range(2):
            ref[i, part, rows, at_lanes(k)] = block[part][k]


def patch_gradients(patches, ext, acc, corners, lives, intensity, probe, waves):
    near, far = patches.near, patches.far

    def lamp(half, row):
        rows = at_rows(half * HALF + row)
        return [[probe[part, rows, at_lanes(k)] for k in range(2)] for part in range(2)]

    def prop(b, row):
        return [waves[part, b, at_rows(row), :] for part in range(2)]

    for i, row in patches.blocks():
        patches.fill(
            i,
            row,
            [
                by_lanes(
                    product, lamp(half, row), patches.window(ext, 0, corners[i], half * HALF + row)
                )
                for half in range(2)
            ],
        )
        if patches.last(row):
            yield
    yield from patches.to_frequencies()
    yield from patches.change(lambda i, b, row, z: product(prop(b, row), z))
    yield from patches.from_frequencies()
    for i, row in patches.blocks():
        leaving = []
        for half in range(2):
            arrived = patches.result(i, half, row)
            second = patches.window(ext, 1, corners[i], half * HALF + row)
            keep_block(near, i, half, row, arrived)
            keep_block(far, i, half, row, second)
            leaving.append(by_lanes(product, second, arrived))
        patches.fill(i, row, leaving)
        if patches.last(row):
            yield
    yield from patches.to_frequencies()

    def residual(i, b, row, z):
        misfit = z[0] * z[0] + z[1] * z[1] - intensity[at_rows(i * PATCH + row), at_lanes(b)]
        return misfit * z[0], misfit * z[1]

    yield from patches.change(residual)
    yield from patches.from_frequencies()
    for i, row in patches.blocks():
        through = []
        for half in range(2):
            back = patches.result(i, half, row)
            start = half * HALF + row
            grad = by_lanes(conj_product, block_of(near, i, half, row), back)
            patches.deposit(acc, 1, corners[i], start, grad, lives[i])
            through.append(by_lanes(conj_product, block_of(far, i, half, row), back))
        patches.fill(i, row, through)
        if patches.last(row):
            yield
    yield from patches.to_frequencies()
    yield from patches.change(lambda i, b, row, z: conj_product(prop(b, row), z))
    yield from patches.from_frequencies()
    for i, row in patches.blocks():
        for half in range(2):
            grad = by_lanes(conj_product, lamp(half, row), patches.result(i, half, row))
            patches.deposit(acc, 0, corners[i], half * HALF + row, grad, lives[i])
        if patches.last(row):
            yield


def in_turns(first, second):
    for _ in range(GROUP // 2):
        next(first)
    going = [first, second]
    while going:
        for group in list(going):
            try:
                next(group)
            except StopIteration:
                going.remove(group)


def place_of(height):
    shard_count = lax.axis_size("scan")
    scan_at = lax.axis_index("scan")
    band = height // shard_count
    upper = scan_at < shard_count // 2
    even = scan_at % 2 == 0
    open_at = jnp.where(upper, HALO, 0)
    shut_at = jnp.where(upper, 0, band - HALO)
    other_at = jnp.where(even, band, 0)
    return [
        jnp.where(upper, 0, height // 2),
        jnp.where(upper, height, -HALO),
        lax.axis_index("row") % 2,
        lax.axis_index("col") % 2,
        jnp.where(even, 0, band),
        other_at + open_at,
        other_at + shut_at,
        ((scan_at == 0) | (scan_at == shard_count - 1)).astype(jnp.int32),
        shut_at,
        open_at,
    ]


def wanted(place, row, half_rows):
    inner = (row < place[0] + half_rows) & (row + PATCH > place[0])
    outer = (row < place[1] + HALO) & (row + PATCH > place[1])
    return inner | outer


def far_tile(place, phase, tiles):
    return jnp.where(place[3] == phase, tiles - 1, 0)


class Copies:
    def __init__(self, sems):
        self.sems, self.all = sems, []

    def start(self, source, target):
        copy = pltpu.make_async_copy(source, target, self.sems.at[len(self.all)])
        copy.start()
        self.all.append(copy)
        return copy

    def wait(self):
        for copy in self.all:
            copy.wait()


def staging_kernel(sides, _, core, *refs):
    col_refs, refs = refs[:sides], refs[sides:]
    cosine, sine, order, near, (ext, waves, *near_to), sems = *refs[:3], refs[3:7], refs[7:-1], refs[-1]
    for k, wave in enumerate((cosine, sine)):
        sorted_wave = sort_frequencies([wave[...]], order)
        for odd in range(2):
            waves[k, odd] = sorted_wave[:, odd * HALF : (odd + 1) * HALF]
    height, width = core.shape[1], core.shape[2]
    tiles = ext.shape[1]
    place = place_of(height)
    copies = Copies(sems)
    for t in range(width // LANE):
        part = core.at[:, :, pl.ds(t * LANE, LANE)]
        copies.start(part, ext.at[:, t + 1, pl.ds(HALO, height), :])
    for source, target in zip(near, near_to):
        copies.start(source, target)
    for j, ref in enumerate(col_refs):
        tile = far_tile(place, j, tiles)
        for p in range(2):
            for k, half in enumerate(unpacked(ref[p], place[3] != j)):
                ext[p + 2 * k, tile, HALO : HALO + height, :] = half
    copies.wait()


def ready_kernel(sides, *refs):
    row_refs, refs = refs[: sides[0]], refs[sides[0] :]
    corner_refs, (_, ext, acc, ends, sems) = refs[: sides[1]], refs[sides[1] :]
    tiles, height = ext.shape[1], ext.shape[2] - 2 * HALO
    place = place_of(height)
    copies = Copies(sems)

    def far_row(phase):
        return pl.ds(pl.multiple_of(jnp.where(place[2] == phase, height + HALO, 0), 8), HALO)

    for i, ref in enumerate(row_refs):
        for t in range(tiles - 2):
            part = ref.at[:, :, pl.ds(t * LANE, LANE)]
            copies.start(part, ext.at[:, t + 1, far_row(i), :])
    for j, ref in enumerate(corner_refs):
        tile = far_tile(place, j, tiles)
        for i in range(sides[0]):
            for p in range(2):
                for q, half in enumerate(unpacked(ref[i, p], place[3] != j)):
                    ends[i, j, p + 2 * q] = half
            copies.start(ends.at[i, j], ext.at[:, tile, far_row(i), :])
    for start, count in ((place[0], height // 2), (place[1], HALO)):
        rows = pl.ds(pl.multiple_of(start + HALO, 8), count)
        acc[:, :, rows, :] = jnp.zeros((4, tiles, count, LANE), jnp.float32)
    copies.wait()


def patches_kernel(cuts, peer, *refs):
    own_info, peer_info, ext, acc, own, probe, waves, tables, order = refs[:9]
    outs, (queue, *scratch, ordered, sems) = refs[10:-15], refs[-15:]
    groups = [Patches(*scratch[:6], tables), Patches(*scratch[6:], tables)]
    tiles, height = ext.shape[1], ext.shape[2] - 2 * HALO
    half_rows = height // 2
    place = place_of(height)
    first = pl.multiple_of(place[0] + HALO, 8)
    outer = pl.multiple_of(place[1] + HALO, 8)

    def intensity(index):
        mine, theirs = jnp.minimum(index, PMAX - 1), jnp.maximum(index - PMAX, 0)
        return jnp.where(index < PMAX, own[mine], peer[theirs])

    length = jnp.int32(0)
    for index in range(2 * PMAX):
        info, slot = (own_info, index) if index < PMAX else (peer_info, index - PMAX)
        row, col, count = info[slot], info[PMAX + slot], info[2 * PMAX]
        queue[3 * length] = index
        queue[3 * length + 1] = row
        queue[3 * length + 2] = col
        length = length + ((slot < count) & wanted(place, row, half_rows)).astype(jnp.int32)

    def step(turn_at, carry):
        start = GROUP * turn_at
        items = [start] + [jnp.minimum(start + i, length - 1) for i in range(1, GROUP)]
        corners = [(queue[3 * i + 1], queue[3 * i + 2]) for i in items]
        lives = [start + i < length for i in range(GROUP)]
        ordered[...] = sort_frequencies([intensity(queue[3 * i]) for i in items], order)
        steps = []
        for k, patches in enumerate(groups):
            part = slice(k * patches.count, (k + 1) * patches.count)
            intensities = ordered.at[pl.ds(k * patches.count * PATCH, patches.count * PATCH)]
            steps.append(
                patch_gradients(
                    patches, ext, acc, corners[part], lives[part], intensities, probe, waves
                )
            )
        in_turns(*steps)
        return carry

    lax.fori_loop(0, (length + GROUP - 1) // GROUP, step, 0)
    gifts = Copies(sems)
    for target, parts in zip(outs, cuts):
        row_to = 0
        for tile, at, count in parts:
            tile = far_tile(place, tile[0], tiles) if isinstance(tile, tuple) else tile
            row = outer if at == OUTER else first
            row = row if at in (OUTER, None) else pl.multiple_of(first + place[at], 8)
            gifts.start(
                acc.at[:, pl.ds(tile, target.shape[1]), pl.ds(row, count), :],
                target.at[:, :, pl.ds(row_to, count), :],
            )
            row_to += count
    gifts.wait()


def near_tile(place, phase, tiles):
    return jnp.where(place[3] == phase, tiles - 1, 0)


def add_rims(place, out, rims, rim_row):
    _, tiles, rows, _ = out.shape
    for j, rim in enumerate(rims):
        at = near_tile(place, j, tiles)
        out[:, at, :, :] += rim[:, 0, pl.ds(rim_row, rows), :]


def edge_kernel(height, sides, open_left, open_right, outer_left, outer_right, *refs):
    place = place_of(height)
    rims, (open_out, outer_out) = refs[:sides], refs[-2:]
    open_out[:, 0:1] = open_left[...]
    open_out[:, 1:] = open_right[...]
    add_rims(place, open_out, rims, pl.multiple_of(place[5], 8))
    outer_out[:, 0:1] = outer_left[...]
    outer_out[:, 1:2] = outer_right[...]
    add_rims(place, outer_out, rims, height // 2)


def shut_inner_kernel(height, part, strip, out):
    place = place_of(height)
    out[...] = part[...]

    @pl.when(place[7] == 0)
    def _():
        out[...] += strip[...]


def shut_edge_kernel(height, sides, left, right, strip, *refs):
    place = place_of(height)
    rims, out = refs[:sides], refs[sides]
    out[:, 0:1] = left[...]
    out[:, 1:2] = right[...]
    add_rims(place, out, rims, pl.multiple_of(place[6], 8))

    @pl.when(place[7] == 0)
    def _():
        out[...] += strip[...]


def gather_kernel(height, sides, part, *refs):
    place = place_of(height)
    shut_got, open_got, strip, rims = refs[0], refs[1:3], refs[3:5], refs[5 : 5 + sides]
    out, edge_out, work = refs[5 + sides :]
    work[...] = part[...]
    tiles = work.shape[1]
    add_rims(place, work, rims, pl.multiple_of(place[4], 8))

    def add(at, inner, edge=None):
        rows = pl.ds(pl.multiple_of(at, 8), inner.shape[2])
        split = 1 + inner.shape[1]
        work[:, 1:split, rows, :] += inner[...]
        if edge is not None:
            work[:, 0:1, rows, :] += edge[:, 0:1]
            work[:, split:, rows, :] += edge[:, 1:]

    add(place[9], *open_got)
    add(place[8], shut_got)

    @pl.when(place[7] == 1)
    def _():
        add(place[8], *strip)

    shut_rows = pl.ds(pl.multiple_of(place[8], 8), HALO)
    edge_out[:, 0:1] = work[:, 0:1, shut_rows, :]
    edge_out[:, 1:2] = work[:, tiles - 1 :, shut_rows, :]
    for t in range(tiles):
        out[:, :, t * LANE : (t + 1) * LANE] = work[:, t]


def last_kernel(height, total, edge, got, out, work, sems):
    place = place_of(height)
    rows = pl.ds(pl.multiple_of(place[8], 8), HALO)
    work[...] = edge[...] + got[...]
    copies = Copies(sems)
    for k in range(2):
        lanes = pl.ds(k * (out.shape[2] - LANE), LANE)
        copies.start(work.at[:, k], out.at[:, rows, lanes])
    copies.wait()


def half_kernel(height, sides, part, inner, edge, *refs):
    place = place_of(height)
    rims, out = refs[:sides], refs[sides]
    out[...] = part[...]
    add_rims(place, out, rims, 0)
    tiles = out.shape[1]
    rows = pl.ds(pl.multiple_of(jnp.where(place[0] == 0, 0, out.shape[2] - HALO), 8), HALO)
    out[:, 1 : tiles - 1, rows, :] += inner[...]
    out[:, 0:1, rows, :] += edge[:, 0:1]
    out[:, tiles - 1 : tiles, rows, :] += edge[:, 1:2]


def near_rows(place, phase, height):
    return pl.ds(pl.multiple_of(jnp.where(place[2] == phase, height - HALO, 0), HALO), HALO)


def near_cols(place, phase, width):
    return pl.ds(pl.multiple_of(jnp.where(place[3] == phase, width - LANE, 0), LANE), LANE)


def sort_frequencies(arrays, order):
    values = side(arrays, 1)
    total = None
    for _ in range(3):
        part = values.astype(jnp.bfloat16)
        values = values - part.astype(jnp.float32)
        rows = times(order[1], part).astype(jnp.bfloat16)
        rows = side([rows[:, i * PATCH : (i + 1) * PATCH] for i in range(len(arrays))], 0)
        moved = times(rows, order[0])
        total = moved if total is None else total + moved
    return total


def packed(strips, high):
    low_lanes = lax.broadcasted_iota(jnp.int32, strips[0].shape, 1) < HALO
    turns = [jnp.where(high, LANE - HALO, 0), jnp.where(high, 0, HALO)]
    parts = [pltpu.roll(strip, turn, 1) for strip, turn in zip(strips, turns)]
    return jnp.where(low_lanes, *parts)


def unpacked(tile, high):
    return [
        pltpu.roll(tile, turn, 1)
        for turn in (jnp.where(high, HALO, 0), jnp.where(high, 0, LANE - HALO))
    ]


def edges_kernel(sides, core, *refs):
    outs, (cols, sems) = refs[:-2], refs[-2:]
    copies = Copies(sems)
    height, width = core.shape[1:]
    place = place_of(height)
    for j in range(sides[1]):
        copies.start(core.at[:, :, near_cols(place, j, width)], cols.at[j])
    for i in range(sides[0]):
        copies.start(core.at[:, near_rows(place, i, height), :], outs[i])
    copies.wait()
    for j in range(sides[1]):
        high = place[3] == j
        for p in range(2):
            outs[sides[0] + j][p] = packed([cols[j, p], cols[j, p + 2]], high)


def corners_kernel(sides, _, *refs):
    strips, outs = refs[: sides[0]], refs[sides[0] :]
    width = strips[0].shape[2]
    for j, out in enumerate(outs):
        high = lax.axis_index("col") % 2 == j
        cols = pl.ds(pl.multiple_of(jnp.where(high, width - LANE, 0), LANE), LANE)
        for i, strip in enumerate(strips):
            for p in range(2):
                out[i, p] = packed([strip[p, :, cols], strip[p + 2, :, cols]], high)


ANY = pl.BlockSpec(memory_space=pl.ANY)
VMEM = pl.BlockSpec(memory_space=pltpu.VMEM)
SMEM = pl.BlockSpec(memory_space=pltpu.SMEM)


def block(*shape):
    return jax.ShapeDtypeStruct(shape, jnp.float32)


def call(kernel, out_shapes, in_specs, out_specs, scratch, *operands, limit=VMEM_LIMIT, aliases=None):
    return pl.pallas_call(
        kernel,
        out_shape=out_shapes,
        in_specs=in_specs,
        out_specs=out_specs,
        scratch_shapes=scratch,
        input_output_aliases=aliases or {},
        compiler_params=pltpu.CompilerParams(vmem_limit_bytes=limit),
        cost_estimate=pl.CostEstimate(flops=0, bytes_accessed=0, transcendentals=0),
    )(*operands)


def shards(object_field, probe_field, prop_phase, measured, positions, counts):
    height, width = object_field.shape[2:]
    shard_count = lax.axis_size("scan")
    half_rows = height // 2
    band = height // shard_count
    rest = band - HALO
    tiles = width // LANE
    row_sides = pairings(lax.axis_size("row"))
    col_sides = pairings(lax.axis_size("col"))
    sides = len(col_sides)
    both = (len(row_sides), sides)
    stride = shard_count // 2
    scan_at = lax.axis_index("scan")
    planes = object_field.reshape(4, height, width)
    own = measured.reshape(PMAX, PATCH, PATCH)
    order = sorted_columns()
    own_info = jnp.concatenate(
        [positions.reshape(PMAX, 2).T.reshape(-1), counts.reshape(1), jnp.zeros((1,), jnp.int32)]
    ).astype(jnp.int32)

    def across(value):
        return lax.ppermute(value, "scan", [(i, i ^ stride) for i in range(shard_count)])

    def to_cols(value, j):
        return joint_permute(value, ("col",), lambda c: (pair_of(c, j),))

    def to_rows(value, i):
        return joint_permute(value, ("row",), lambda r: (pair_of(r, i),))

    peer = across(own)
    peer_info = across(own_info)
    edge_shapes = (
        [block(4, HALO, width)] * both[0]
        + [block(2, height, LANE)] * sides
    )
    edges = call(
        functools.partial(edges_kernel, both),
        edge_shapes,
        [ANY],
        [VMEM] * len(edge_shapes),
        [pltpu.VMEM((sides, 4, height, LANE), jnp.float32), pltpu.SemaphoreType.DMA((sum(both),))],
        planes,
        limit=VMEM_LITTLE,
    )
    row_halos = [to_rows(edges[i], i) for i in row_sides]
    col_halos = [to_cols(edges[both[0] + j], j) for j in col_sides]
    cosine, sine = jnp.cos(prop_phase), jnp.sin(prop_phase)
    tables = block_tables()

    two_bands = shard_count == 4 and rest > 0
    inner = tiles - 2
    cuts = [(inner, [(2, OUTER, HALO)]), (1, [(1, OUTER, HALO)]), (1, [(tiles, OUTER, HALO)])]
    cuts += [(1, [((j,), None, half_rows), ((j,), OUTER, HALO)]) for j in col_sides]
    if two_bands:
        early = inner
        right = tiles - early - 1
        cuts += [(early, [(2, 5, rest)]), (1, [(1, 5, rest)]), (right, [(2 + early, 5, rest)])]
        cuts += [(inner, [(2, 6, HALO)]), (1, [(1, 6, HALO)]), (1, [(tiles, 6, HALO)])]
        cuts += [(tiles, [(1, 4, band)])]
    else:
        cuts += [(tiles, [(1, None, half_rows)]), (1, [(1, None, HALO)]), (1, [(1, None, HALO)])]
    full = (4, tiles + 2, height + 2 * HALO, LANE)
    ext, waves, lamp, near_tables, near_own, near_order = call(
        functools.partial(staging_kernel, sides),
        [
            block(*full),
            block(2, 2, PATCH, HALF),
            block(*probe_field.shape),
            jax.ShapeDtypeStruct(tables.shape, tables.dtype),
            block(*own.shape),
            jax.ShapeDtypeStruct(order.shape, order.dtype),
        ],
        [SMEM, ANY] + [VMEM] * (sides + 3) + [ANY] * 4,
        [VMEM] * 6,
        [pltpu.SemaphoreType.DMA((tiles + 4,))],
        own_info,
        planes,
        *col_halos,
        cosine,
        sine,
        order,
        probe_field,
        tables,
        own,
        order,
        limit=VMEM_LITTLE,
    )
    row_ends = call(
        functools.partial(corners_kernel, both),
        [block(both[0], 2, HALO, LANE)] * sides,
        [VMEM] * (1 + both[0]),
        [VMEM] * sides,
        [],
        near_order,
        *row_halos,
        limit=VMEM_LITTLE,
    )
    corner_halos = [to_cols(ends, j) for j, ends in zip(col_sides, row_ends)]
    ext, acc = call(
        functools.partial(ready_kernel, both),
        [block(*full), block(*full)],
        [ANY] * both[0] + [VMEM] * sides + [ANY],
        [ANY, VMEM],
        [
            pltpu.VMEM((*both, 4, HALO, LANE), jnp.float32),
            pltpu.SemaphoreType.DMA((both[0] * (tiles + sides),)),
        ],
        *row_halos,
        *corner_halos,
        ext,
        limit=VMEM_LITTLE,
        aliases={both[0] + sides: 0},
    )
    outs = call(
        functools.partial(patches_kernel, [parts for _, parts in cuts]),
        [block(*full)] + [block(4, wide, sum(part[2] for part in parts), LANE) for wide, parts in cuts],
        [VMEM, SMEM, SMEM] + [VMEM] * 7,
        [VMEM] + [ANY] * len(cuts),
        [
            pltpu.SMEM((3 * (2 * PMAX + 1),), jnp.int32),
            *[
                pltpu.VMEM(shape, dtype)
                for _ in range(2)
                for shape, dtype in (
                    ((2, PATCH, GROUP // 2 * PATCH), jnp.bfloat16),
                    ((2, PATCH, GROUP // 2 * PATCH), jnp.float32),
                    ((2, GROUP // 2 * PATCH, PATCH), jnp.bfloat16),
                    ((2, GROUP // 2 * PATCH, PATCH), jnp.float32),
                    ((GROUP // 2, 2, PATCH, PATCH), jnp.float32),
                    ((GROUP // 2, 2, PATCH, PATCH), jnp.float32),
                )
            ],
            pltpu.VMEM((GROUP * PATCH, PATCH), jnp.float32),
            pltpu.SemaphoreType.DMA((sum(len(parts) for _, parts in cuts),)),
        ],
        peer,
        own_info,
        peer_info,
        ext,
        acc,
        near_own,
        lamp,
        waves,
        near_tables,
        near_order,
        aliases={4: 0},
    )[1:]
    outer_inner, outer_left, outer_right = outs[:3]
    rims, pieces = outs[3 : 3 + sides], outs[3 + sides :]

    def to_next(value):
        return joint_permute(
            value, ("row", "scan"), lambda r, s: (r + 1 if s < stride else r - 1, s)
        )

    def beside(value, mask=1):
        return lax.ppermute(value, "scan", [(i, i ^ mask) for i in range(shard_count)])

    def fold(kernel, out_shapes, *operands, scratch=()):
        many = isinstance(out_shapes, tuple)
        return call(
            functools.partial(kernel, height),
            out_shapes,
            [VMEM] * len(operands),
            (VMEM,) * len(out_shapes) if many else VMEM,
            list(scratch),
            *operands,
            limit=VMEM_LITTLE,
        )

    got_rims = [to_cols(rim, j) for j, rim in zip(col_sides, rims)]
    got_inner = to_next(outer_inner)
    open_edge, outer_edge = fold(
        lambda *refs: edge_kernel(refs[0], sides, *refs[1:]),
        (
            block(4, 1 + pieces[2].shape[1], pieces[1].shape[2], LANE),
            block(4, 2, HALO, LANE),
        ),
        pieces[1],
        pieces[2],
        outer_left,
        outer_right,
        *got_rims,
    )
    got_edge = to_next(outer_edge)
    if not two_bands:
        half = fold(
            lambda *refs: half_kernel(refs[0], sides, *refs[1:]),
            block(4, tiles, half_rows, LANE),
            pieces[0],
            got_inner,
            got_edge,
            *got_rims,
        )
        mask = stride // 2
        while mask > 0:
            size = half.shape[2] // 2
            low = (scan_at & mask) == 0
            keep = lax.dynamic_slice_in_dim(half, jnp.where(low, 0, size), size, axis=2)
            send = lax.dynamic_slice_in_dim(half, jnp.where(low, size, 0), size, axis=2)
            half = keep + beside(send, mask)
            mask //= 2
        return half.transpose(0, 2, 1, 3).reshape(2, 2, band, width)
    got_open = [beside(pieces[0]), beside(open_edge)]
    got_open[0], got_inner = lax.optimization_barrier((got_open[0], got_inner))
    got_open[1], got_edge = lax.optimization_barrier((got_open[1], got_edge))
    shut_inner = fold(shut_inner_kernel, block(4, inner, HALO, LANE), pieces[3], got_inner)
    got_shut = [beside(shut_inner)]
    shut_edge = fold(
        lambda *refs: shut_edge_kernel(refs[0], sides, *refs[1:]),
        block(4, 2, HALO, LANE),
        pieces[4],
        pieces[5],
        got_edge,
        *got_rims,
    )
    got_shut.append(beside(shut_edge))
    bulk, shut_rest = fold(
        lambda *refs: gather_kernel(refs[0], sides, *refs[1:]),
        (block(4, band, width), block(4, 2, HALO, LANE)),
        pieces[6],
        got_shut[0],
        *got_open,
        got_inner,
        got_edge,
        *got_rims,
        scratch=[pltpu.VMEM((4, tiles, band, LANE), jnp.float32)],
    )
    total = call(
        functools.partial(last_kernel, height),
        block(4, band, width),
        [ANY, VMEM, VMEM],
        ANY,
        [pltpu.VMEM((4, 2, HALO, LANE), jnp.float32), pltpu.SemaphoreType.DMA((2,))],
        bulk,
        shut_rest,
        got_shut[1],
        limit=VMEM_LITTLE,
        aliases={0: 0},
    )
    return total.reshape(2, 2, band, width)


def solution(mesh):
    placed = (
        P(None, None, "row", "col"),
        P(),
        P(),
        P("row", "col", "scan", None, None, None),
        P("row", "col", "scan", None, None),
        P("row", "col", "scan"),
    )
    return jax.shard_map(
        shards,
        mesh=mesh,
        in_specs=placed,
        out_specs=P(None, None, ("row", "scan"), "col"),
        check_vma=False,
    )
```
